256 devices in a mesh: blk: 16 (over y_hi, z), mer: 8 (over x, core), ply: 2 (over y_lo).
Axes of the slice: x: 4, y: 4 (y_hi: 2, y_lo: 2; y = y_hi * 2 + y_lo), z: 8, core: 2. Of those that a mesh axis runs over, the one named last changes fastest.
Arguments:
- loads: float32 [16, 8, 1536, 128], P('blk', 'mer', 'ply'), may hold values from -6 to 6
- schur: float32 [16, 8, 1536, 1536], P('blk', 'mer', 'ply'), as said below
- local_inverse: float32 [16, 8, 1536, 1536], P('blk', 'mer', 'ply'), as said below
- psi: float32 [16, 8, 1536, 8], P('blk', 'mer', 'ply'), may hold values from -0.21875 to 0.21875
- face_map: int32 [16, 8, 2, 4, 192], P('blk', 'mer', 'ply'), may hold values from 0 to 191, as said below
- primal_list: int32 [16, 8, 2, 8], P('blk', 'mer', 'ply'), may hold values from 0 to 2047, as said below
- coarse_inverse: float32 [2048, 2048], P(('blk', 'mer', 'ply')), as said below
Outputs:
- solution: float32 [16, 8, 1536, 128], P('blk', 'mer', 'ply')
- residual: float32 [16, 8, 1536, 128], P('blk', 'mer', 'ply')
The draws below stay inside these ranges and needn't reach their ends.
Inputs may be any that keep to these rules, and one draw needn't show every extreme that they name: schur is symmetric and positive definite for every substructure. local_inverse is symmetric and positive definite for every substructure. coarse_inverse is symmetric and positive definite. Each face_map[b, m, p, f] is a permutation of 0 to 191; face_map[b, m, p, 0] is the inverse permutation of face_map[b - 1, m, p, 1] (cycle index modulo 16), and face_map[b, m, p, 2] is the inverse of face_map[b, m - 1, p, 3] for m > 0. `primal_list`: coarse unknown o of ply group (b, m, p) is ((b * 8 + m) * 2 + p) * 8 + o; every slot names a coarse unknown of its own ply group or of the ply group with the same m and p at cycle index b - 1 or b + 1 (modulo 16), or with the same b and p at meridian index m - 1 or m + 1.
All inputs are finite; a program needn't handle non-finite values.
Results may differ from the reference program's by a relative error of at most 0.0003.
Values sent between devices are 32-bit elements; how exact they have to be, the bound alone decides.
A program may use at most 64 MiB of HBM per device.

```python
import math
import jax
import jax.numpy as jnp
from jax import lax

NI = 1536
LOADS = 128
PL = 8
CPS = 8
ITERS = 4
CYCLE = 16
MERS = 8
PLIES = 2
HALF = 768
FACE = 192
NC = 2048


def shared_scale(key):
    level = jax.random.uniform(key, (CYCLE, MERS, NI), jnp.float32, 0.0, math.log(4.0))
    return jnp.exp(level)


def symmetric_noise(key, lead, order, power):
    raw = jax.random.uniform(key, lead + (order, order), jnp.float32, -1.0, 1.0)
    raw = jnp.sign(raw) * jnp.abs(raw) ** power
    noise = 0.5 * (raw + jnp.swapaxes(raw, -1, -2))
    return noise * (1.0 - jnp.eye(order, dtype=jnp.float32))


def draw_schur(key, part):
    scale = shared_scale(key)
    key = jax.random.fold_in(key, 11)
    power = 1.0
    noise = symmetric_noise(key, (CYCLE, MERS), NI, power)
    return noise * (1.9 / NI) + jnp.eye(NI, dtype=jnp.float32) * (2.0 * scale)[..., None]


def draw_local_inverse(key, part):
    scale = shared_scale(key)
    key = jax.random.fold_in(key, 12)
    power = 1.0
    noise = symmetric_noise(key, (CYCLE, MERS), NI, power)
    return noise * (0.12 / NI) + jnp.eye(NI, dtype=jnp.float32) * (0.5 / scale)[..., None]


def draw_coarse_inverse(key, part):
    key = jax.random.fold_in(key, 13)
    first, second = jax.random.split(key)
    power = 1.0
    noise = symmetric_noise(first, (), NC, power)
    diagonal = jnp.exp(jax.random.uniform(second, (NC,), jnp.float32, 0.0, math.log(3.0)))
    coupling = jnp.full((NC, NC), 4.0 / NC, jnp.float32)
    return noise * (0.95 / NC) + coupling + jnp.eye(NC, dtype=jnp.float32) * diagonal[:, None]


def random_perms(key):
    scores = jax.random.randint(key, (CYCLE, MERS, PLIES, FACE), 0, 65536) * FACE + jnp.arange(FACE)
    return jnp.argsort(scores, axis=-1).astype(jnp.int32)


def draw_face_map(key, part):
    key = jax.random.fold_in(key, 14)
    first, second = jax.random.split(key)
    cycle_hi = random_perms(first)
    cycle_lo = jnp.roll(jnp.argsort(cycle_hi, axis=-1), 1, axis=0)
    mer_hi = random_perms(second)
    mer_lo = jnp.roll(jnp.argsort(mer_hi, axis=-1), 1, axis=1)
    return jnp.stack([cycle_lo, cycle_hi, mer_lo, mer_hi], axis=3).astype(jnp.int32)


def draw_primal_list(key, part):
    key = jax.random.fold_in(key, 15)
    first, second = jax.random.split(key)
    kinds = jax.random.randint(first, (CYCLE, MERS, PLIES, PL), 0, 5)
    offsets = jax.random.randint(second, (CYCLE, MERS, PLIES, PL), 0, CPS)
    slot_ids = jnp.arange(PL)[None, None, None, :]
    kinds = jnp.where((slot_ids == 0) | (slot_ids == PL - 1), 0, kinds)
    offsets = jnp.where(slot_ids == 0, 0, jnp.where(slot_ids == PL - 1, CPS - 1, offsets))
    cycle_ids = jnp.arange(CYCLE)[:, None, None, None]
    mer_ids = jnp.arange(MERS)[None, :, None, None]
    ply_ids = jnp.arange(PLIES)[None, None, :, None]
    cycle_dst = jnp.where(kinds == 1, (cycle_ids - 1) % CYCLE, jnp.where(kinds == 2, (cycle_ids + 1) % CYCLE, cycle_ids))
    mer_dst = jnp.where((kinds == 3) & (mer_ids > 0), mer_ids - 1, jnp.where((kinds == 4) & (mer_ids < MERS - 1), mer_ids + 1, mer_ids))
    owner = (cycle_dst * MERS + mer_dst) * PLIES + ply_ids
    return (owner * CPS + offsets).astype(jnp.int32)


def block_levels(key, dims, shards, least, high):
    def one(dim, shards_of):
        draws = jax.random.uniform(jax.random.fold_in(jax.random.fold_in(key, 6), dim), (shards_of,), jnp.float32, least / len(shards), high / len(shards))
        return jnp.repeat(jnp.exp(draws), dims[dim] // shards_of).reshape((-1,) + (1,) * (len(dims) - dim - 1))

    gain = one(*shards[0])
    for cut in shards[1:]:
        gain = gain * one(*cut)
    return gain


def centred(stream_key, shape, scale, reach, pieces=(), kind=jnp.bfloat16):
    entries = scale * jax.random.normal(stream_key, shape, jnp.float32)
    if pieces:
        entries = entries * block_levels(stream_key, shape, pieces, -0.22, 0.18)
    return jnp.clip(entries, -reach, reach).astype(kind)


def setup_inputs(seed: int = 0) -> dict:
    splits = jax.random.split(jax.random.key(seed), 8)
    loads = centred(splits[0], (CYCLE, MERS, NI, LOADS), 1.0, 6.0, ((0, 16), (1, 8), (2, 2)), jnp.float32)
    schur = draw_schur(jax.random.fold_in(splits[7], 71), 0)
    local_inverse = draw_local_inverse(jax.random.fold_in(splits[7], 71), 0)
    psi = centred(splits[3], (CYCLE, MERS, NI, PL), HALF ** -0.5, 0.21875, ((0, 16), (1, 8), (2, 2)), jnp.float32)
    face_map = draw_face_map(jax.random.fold_in(splits[7], 71), 0)
    primal_list = draw_primal_list(jax.random.fold_in(splits[7], 71), 0)
    coarse_inverse = draw_coarse_inverse(jax.random.fold_in(splits[7], 71), 0)
    return dict(loads=loads, schur=schur, local_inverse=local_inverse, psi=psi, face_map=face_map, primal_list=primal_list, coarse_inverse=coarse_inverse)


HIGH = lax.Precision.HIGHEST


def face_weights():
    mer_ids = jnp.arange(MERS)[:, None]
    face_ids = jnp.arange(4)[None, :]
    ends = ((face_ids == 2) & (mer_ids == 0)) | ((face_ids == 3) & (mer_ids == MERS - 1))
    weights = jnp.where(ends, 1.0, 0.5).astype(jnp.float32)
    weights = jnp.broadcast_to(weights[None, :, None, :, None], (CYCLE, MERS, PLIES, 4, FACE))
    return weights.reshape(CYCLE, MERS, NI, 1)


def pick_rows(source, links):
    index = jnp.broadcast_to(links[..., None], source.shape)
    return jnp.take_along_axis(source, index, axis=3)


def assemble(vec, face_map):
    split = vec.reshape(CYCLE, MERS, PLIES, 4, FACE, vec.shape[-1])
    prev_hi = jnp.roll(split[:, :, :, 1], 1, axis=0)
    next_lo = jnp.roll(split[:, :, :, 0], -1, axis=0)
    zero = jnp.zeros_like(split[:, :1, :, 0])
    mer_prev = jnp.concatenate([zero, split[:, :-1, :, 3]], axis=1)
    mer_next = jnp.concatenate([split[:, 1:, :, 2], zero], axis=1)
    incoming = jnp.stack([pick_rows(prev_hi, face_map[:, :, :, 0]), pick_rows(next_lo, face_map[:, :, :, 1]),
                          pick_rows(mer_prev, face_map[:, :, :, 2]), pick_rows(mer_next, face_map[:, :, :, 3])], axis=3)
    return (split + incoming).reshape(vec.shape)


def apply_local(matrix, vec):
    return jnp.einsum('bmij,bmjr->bmir', matrix, vec, precision=HIGH)


def inner(weights, left, right):
    return jnp.sum(weights * left * right, axis=(0, 1, 2))


def precondition(residual, weights, local_inverse, psi, face_map, primal_list, coarse_inverse):
    cases = residual.shape[-1]
    scaled = weights * residual
    local_part = apply_local(local_inverse, scaled)
    basis = psi.reshape(CYCLE, MERS, PLIES, HALF, PL)
    terms = jnp.einsum('bmphk,bmphr->bmpkr', basis, scaled.reshape(CYCLE, MERS, PLIES, HALF, cases), precision=HIGH)
    coarse_rhs = jnp.zeros((NC, cases), jnp.float32).at[primal_list.reshape(-1)].add(terms.reshape(-1, cases))
    coarse_x = jnp.dot(coarse_inverse, coarse_rhs, precision=HIGH)
    picked = coarse_x[primal_list]
    correction = jnp.einsum('bmphk,bmpkr->bmphr', basis, picked, precision=HIGH).reshape(residual.shape)
    return assemble(weights * (local_part + correction), face_map)


def reference(loads, schur, local_inverse, psi, face_map, primal_list, coarse_inverse):
    weights = face_weights()
    solution = jnp.zeros_like(loads)
    residual = assemble(loads, face_map)
    precond = precondition(residual, weights, local_inverse, psi, face_map, primal_list, coarse_inverse)
    direction = precond
    rz = inner(weights, residual, precond)
    for step in range(ITERS):
        image = assemble(apply_local(schur, direction), face_map)
        alpha = rz / inner(weights, direction, image)
        solution = solution + alpha * direction
        residual = residual - alpha * image
        if step + 1 < ITERS:
            precond = precondition(residual, weights, local_inverse, psi, face_map, primal_list, coarse_inverse)
            rz_new = inner(weights, residual, precond)
            direction = precond + (rz_new / rz) * direction
            rz = rz_new
    return solution, residual
```

```python
import functools

import jax
import jax.numpy as jnp
from jax import lax
from jax.experimental import pallas as pl
from jax.experimental.pallas import tpu as pltpu
from jax.sharding import PartitionSpec as P

ITERS = 4
EXCH = 2 * ITERS + 1
F32 = jnp.float32
BF16 = jnp.bfloat16
HIGH = lax.Precision.HIGHEST
MESH = pl.DeviceIdType.MESH
NT = (((1,), (1,)), ((), ()))


def halves(value):
    hi = value.astype(BF16)
    return hi, (value - hi.astype(F32)).astype(BF16)


def thirds(value):
    hi = value.astype(BF16)
    rest = value - hi.astype(F32)
    mid = rest.astype(BF16)
    return hi, mid, (rest - mid.astype(F32)).astype(BF16)


def dot(left, right):
    return jnp.dot(left, right, preferred_element_type=F32)


def remote(src, dst, send, recv, device):
    return pltpu.make_async_remote_copy(
        src_ref=src, dst_ref=dst, send_sem=send, recv_sem=recv, device_id=device, device_id_type=MESH
    )


def kernel(
    sizes,
    loads_ref, schur_ref, linv_ref, psi_ref, map_ref, list_ref, coarse_ref,
    x_ref, r_ref,
    lf, sf, lhi, llo, shi, slo,
    face_tx, face_rx, own, ply_rx,
    other, pdir, sraw, acc, gvec, tb, perm, psc, pst,
    nbr, dpad, wblk, cblk, lists,
    co1, ytx, co2, ar1, ar2, rz_ref,
    load_sem, face_ss, face_rs, ply_ss, ply_rs,
    nbr_ss, nbr_rs, win_ss, win_rs, list_ss, list_rs,
    co1_ss, co1_rs, co2_ss, co2_rs, ar1_ss, ar1_rs, ar2_ss, ar2_rs,
):
    nb, nm, npl = sizes
    ng = nm * npl
    half, cases = loads_ref.shape
    face = half // 4
    owned = coarse_ref.shape[0]
    b = lax.axis_index("blk")
    m = lax.axis_index("mer")
    p = lax.axis_index("ply")
    q = 1 - p
    mp = m * npl + p
    b_prev = lax.rem(b + nb - 1, nb)
    b_next = lax.rem(b + 1, nb)
    has_lo = m > 0
    has_hi = m < nm - 1
    weight = [
        0.5,
        0.5,
        jnp.where(has_lo, 0.5, 1.0).astype(F32),
        jnp.where(has_hi, 0.5, 1.0).astype(F32),
    ]
    partner = (b, m, q)
    neighbour = [(b_prev, m, p), (b_next, m, p), (b, m - 1, p), (b, m + 1, p)]
    exists = [None, None, has_lo, has_hi]

    def guarded(f, fn):
        if exists[f] is None:
            fn()
        else:
            pl.when(exists[f])(fn)

    def mp_device(index):
        return (b, lax.div(index, npl), lax.rem(index, npl))

    def blk_device(index):
        return (index, m, p)

    def spread(count, me, device_of, src_of, dst, send, recv):
        def step(j, carry):
            peer = lax.rem(me + j, count)
            remote(src_of(peer), dst, send, recv, device_of(peer)).start()
            return carry

        lax.fori_loop(1, count, step, 0)

    def fetch(index, source, side, target):
        column = pl.multiple_of(side * half, 128)
        return pltpu.make_async_copy(
            source.at[:, pl.ds(column, half)], target.at[index % 2], load_sem.at[index]
        )

    fetches = [
        fetch(0, linv_ref, p, lf),
        fetch(1, linv_ref, q, lf),
        fetch(2, schur_ref, p, sf),
        fetch(3, schur_ref, q, sf),
    ]
    for copy in fetches:
        copy.start()

    barrier = pltpu.get_barrier_semaphore()

    def greet(count, me, device_of):
        def step(j, carry):
            peer = lax.rem(me + j, count)
            pl.semaphore_signal(barrier, inc=1, device_id=device_of(peer), device_id_type=MESH)
            return carry

        lax.fori_loop(1, count, step, 0)

    greet(ng, mp, mp_device)
    greet(nb, b, blk_device)

    rows = lax.broadcasted_iota(jnp.int32, (face, face), 0)
    for f in range(4):
        perm[f] = jnp.where(rows == map_ref[f : f + 1, :], 1.0, 0.0).astype(BF16)

    for f in (2, 3):

        @pl.when(jnp.logical_not(exists[f]))
        def _():
            def clear(e, carry):
                face_rx[e, f] = jnp.zeros((face, cases), F32)
                return carry

            lax.fori_loop(0, EXCH, clear, 0)
            nbr[1 + f] = jnp.zeros(nbr.shape[1:], F32)

    lane = lax.broadcasted_iota(jnp.int32, (owned, lists.shape[2]), 1)
    sub = lax.broadcasted_iota(jnp.int32, (owned, lists.shape[2]), 0)
    mine = jnp.zeros_like(lane)
    for k in range(owned):
        mine = jnp.where(sub == k, list_ref[k], mine)
    lists[mp] = mine

    def permute(f, value):
        hi, mid, lo = thirds(value)
        out = dot(perm[f], jnp.concatenate([hi, mid, lo], axis=1))
        return (out[:, 2 * cases :] + out[:, cases : 2 * cases]) + out[:, :cases]

    def face_copy(e, f):
        return remote(
            face_tx.at[e, f], face_rx.at[e, f ^ 1], face_ss.at[e, f], face_rs.at[e, f ^ 1], neighbour[f]
        )

    def face_send(e, f, value):
        def go():
            face_tx[e, f] = permute(f, value)
            face_copy(e, f).start()

        guarded(f, go)

    def face_wait(e, f):
        guarded(
            f,
            lambda: remote(
                face_tx.at[e, f], face_rx.at[e, f], face_ss.at[e, f], face_rs.at[e, f], neighbour[f]
            ).wait_recv(),
        )

    def faces_sent(e):
        for f in range(4):
            guarded(f, lambda f=f: face_copy(e, f).wait_send())

    def ply_copy(e, pair):
        part = pl.ds(2 * pair, 2)
        return remote(own.at[e, part], ply_rx.at[e, part], ply_ss.at[e, pair], ply_rs.at[e, pair], partner)

    def batch(buffer, index, count, send, recv):
        block = buffer.at[index, pl.ds(0, count - 1)]
        return remote(block, block, send, recv, partner)

    def reduce_first(k, value):
        ar1[k, mp] = value
        spread(ng, mp, mp_device, lambda _: ar1.at[k, mp], ar1.at[k, mp], ar1_ss.at[k], ar1_rs.at[k])

    def reduce_second(k):
        batch(ar1, k, ng, ar1_ss.at[k], ar1_rs.at[k]).wait_recv()
        ar2[k, b] = jnp.sum(ar1[k], axis=0)
        spread(nb, b, blk_device, lambda _: ar2.at[k, b], ar2.at[k, b], ar2_ss.at[k], ar2_rs.at[k])

    def reduce_end(k):
        batch(ar2, k, nb, ar2_ss.at[k], ar2_rs.at[k]).wait_recv()
        return jnp.sum(ar2[k], axis=0)

    def reduce_sent(k):
        batch(ar1, k, ng, ar1_ss.at[k], ar1_rs.at[k]).wait_send()
        batch(ar2, k, nb, ar2_ss.at[k], ar2_rs.at[k]).wait_send()

    def store_split(side, f, value):
        hi, lo = halves(value)
        part = pl.ds(f * face, face)
        tb[side, part, pl.ds(0, cases)] = hi
        tb[side, part, pl.ds(cases, cases)] = lo

    def product(hi, lo, side):
        both = dot(hi[side], tb[side])
        small = dot(lo[side], tb[side, :, pl.ds(0, cases)])
        return (both[:, :cases] + both[:, cases:]) + small

    pl.semaphore_wait(barrier, ng - 1 + nb - 1)

    for f in (0, 1, 2, 3):
        face_send(0, f, loads_ref[pl.ds(f * face, face), :])

    slot_there = [2, 1, 4, 3]

    def nbr_copy(f):
        slot = slot_there[f]
        return remote(coarse_ref, nbr.at[slot], nbr_ss.at[f], nbr_rs.at[slot - 1], neighbour[f])

    for f in range(4):
        guarded(f, lambda f=f: nbr_copy(f).start())
    nbr[0] = coarse_ref[...]
    spread(ng, mp, mp_device, lambda _: lists.at[mp], lists.at[mp], list_ss.at[0], list_rs.at[0])

    psi = psi_ref[...]
    psi_hi, psi_lo = halves(psi)
    psi_hi = psi_hi.astype(F32)
    psc[...] = jnp.concatenate([psi_hi, psi_hi, psi_lo.astype(F32)], axis=1).astype(BF16)
    pick_r = lax.broadcasted_iota(jnp.int32, (2 * owned, 3 * owned), 0)
    pick_c = lax.broadcasted_iota(jnp.int32, (2 * owned, 3 * owned), 1)
    want = jnp.where(pick_r < owned, pick_r, pick_r + owned)
    pick = jnp.where(want == pick_c, 1.0, 0.0).astype(BF16)
    pst[...] = lax.dot_general(pick, psc[...], NT, preferred_element_type=F32).astype(BF16)

    def split_matrix(source, hi, lo):
        def step(i, carry):
            part = pl.ds(i * 64, 64)
            for side in range(2):
                a, c = halves(source[side, part, :])
                hi[side, part, :] = a
                lo[side, part, :] = c
            return carry

        lax.fori_loop(0, half // 64, step, 0)

    fetches[0].wait()
    fetches[1].wait()
    split_matrix(lf, lhi, llo)

    group = ng * owned
    this = (b * nm + m) * npl + p
    bases = [
        this * owned,
        ((b_prev * nm + m) * npl + p) * owned,
        ((b_next * nm + m) * npl + p) * owned,
        jnp.where(has_lo, (this - npl) * owned, -owned),
        jnp.where(has_hi, (this + npl) * owned, -owned),
    ]
    wide = lax.broadcasted_iota(jnp.int32, (owned, 5 * owned), 1)
    tall = lax.broadcasted_iota(jnp.int32, (owned, 5 * owned), 0)
    names = jnp.zeros_like(wide)
    for t in range(5):
        names = jnp.where(lax.div(wide, owned) == t, bases[t] + wide - t * owned, names)
    slots = jnp.zeros_like(wide)
    for k in range(owned):
        slots = jnp.where(tall == k, list_ref[k], slots)
    selector = jnp.where(slots == names, 1.0, 0.0).astype(F32)
    for f in range(4):
        guarded(
            f,
            lambda f=f: remote(
                coarse_ref, nbr.at[1 + f], nbr_ss.at[f], nbr_rs.at[f], neighbour[f]
            ).wait_recv(),
        )
    named = jnp.dot(
        selector, nbr[...].reshape(5 * owned, nbr.shape[2]), precision=HIGH, preferred_element_type=F32
    )
    for j in range(nb + 2):
        block = (j - 1) % nb
        dpad[j] = named[:, block * group : (block + 1) * group]
    wblk[b] = dpad[pl.ds(b, 3)]
    spread(nb, b, blk_device, lambda peer: dpad.at[pl.ds(peer, 3)], wblk.at[b], win_ss.at[0], win_rs.at[0])

    for f in (2, 3, 0, 1):
        face_wait(0, f)
        value = loads_ref[pl.ds(f * face, face), :] + face_rx[0, f]
        own[0, f] = value
        r_ref[pl.ds(f * face, face), :] = value
        other[f] = jnp.zeros((face, cases), F32)
        if f in (3, 1):
            ply_copy(0, f // 2).start()
    x_ref[...] = jnp.zeros_like(x_ref)
    pdir[...] = jnp.zeros_like(pdir)
    sraw[...] = jnp.zeros_like(sraw)
    rz_ref[...] = jnp.ones_like(rz_ref)

    block = lists.at[pl.ds(0, ng - 1)]
    remote(block, block, list_ss.at[0], list_rs.at[0], partner).wait_recv()
    names = lists[:, :, pl.ds(0, group)].reshape(group, group)
    column = lax.broadcasted_iota(jnp.int32, (group, group), 1)
    block = wblk.at[pl.ds(0, nb - 1)]
    remote(block, block, win_ss.at[0], win_rs.at[0], partner).wait_recv()
    total = jnp.zeros((nb * owned, group), F32)
    for j, start in enumerate((b_prev, b, b_next)):
        hot = jnp.where(names == column + start * group, 1.0, 0.0).astype(F32)
        window = wblk[:, j].reshape(nb * owned, group)
        total += lax.dot_general(window, hot, NT, precision=HIGH, preferred_element_type=F32)
    cblk[...] = total

    for f in range(4):
        guarded(f, lambda f=f: nbr_copy(f).wait_send())
    block = lists.at[pl.ds(0, ng - 1)]
    remote(block, block, list_ss.at[0], list_rs.at[0], partner).wait_send()
    block = wblk.at[pl.ds(0, nb - 1)]
    remote(block, block, win_ss.at[0], win_rs.at[0], partner).wait_send()
    faces_sent(0)

    def iteration(it, alpha):
        e1 = 1 + 2 * it
        e2 = 2 + 2 * it
        k1 = 2 * it
        k2 = 2 * it + 1

        for f in range(4):
            store_split(0, f, weight[f] * r_ref[pl.ds(f * face, face), :])
        parts = dot(pst[...], tb[0])
        terms = parts[:owned, :cases] + parts[:owned, cases:] + parts[owned:, :cases]
        co1[it, mp] = terms
        spread(ng, mp, mp_device, lambda _: co1.at[it, mp], co1.at[it, mp], co1_ss.at[it], co1_rs.at[it])
        acc[...] = product(lhi, llo, 0)

        batch(co1, it, ng, co1_ss.at[it], co1_rs.at[it]).wait_recv()
        y = jnp.dot(
            cblk[...], co1[it].reshape(group, cases), precision=HIGH, preferred_element_type=F32
        )
        ytx[it] = y.reshape(nb, owned, cases)
        spread(nb, b, blk_device, lambda peer: ytx.at[it, peer], co2.at[it, b], co2_ss.at[it], co2_rs.at[it])
        co2[it, b] = ytx[it, b]

        @pl.when(it == 0)
        def _():
            fetches[2].wait()
            fetches[3].wait()
            split_matrix(sf, shi, slo)

        for f in (2, 3, 0, 1):
            if f in (2, 0):
                ply_copy(e1 - 1, f // 2).wait_recv()
            value = other[f] + alpha * ply_rx[e1 - 1, f]
            other[f] = value
            store_split(1, f, weight[f] * value)
        acc[...] += product(lhi, llo, 1)

        batch(co2, it, nb, co2_ss.at[it], co2_rs.at[it]).wait_recv()
        picked = jnp.sum(co2[it], axis=0)
        pick_hi = picked.astype(BF16).astype(F32)
        stack = jnp.concatenate([pick_hi, picked - pick_hi, pick_hi], axis=0).astype(BF16)
        acc[...] += dot(psc[...], stack)

        partial = jnp.zeros((8, cases), F32)
        for f in (0, 1, 2, 3):
            part = pl.ds(f * face, face)
            value = weight[f] * acc[part, :]
            gvec[f] = value
            face_send(e1, f, value)
            partial += jnp.sum((value * r_ref[part, :]).reshape(face // 8, 8, cases), axis=0)
        reduce_first(k1, jnp.sum(partial, axis=0, keepdims=True))

        for f in (2, 3, 0, 1):
            face_wait(e1, f)
            value = gvec[f] + face_rx[e1, f]
            own[e1, f] = value
            if f in (3, 1):
                ply_copy(e1, f // 2).start()
            store_split(0, f, value)
        reduce_second(k1)

        acc[...] = product(shi, slo, 0)
        rz = reduce_end(k1)
        beta = jnp.where(it == 0, 0.0, rz / rz_ref[...])
        rz_ref[...] = rz
        for f in range(4):
            pdir[f] = own[e1, f] + beta * pdir[f]
        batch(co1, it, ng, co1_ss.at[it], co1_rs.at[it]).wait_send()
        batch(co2, it, nb, co2_ss.at[it], co2_rs.at[it]).wait_send()
        reduce_sent(k1)
        faces_sent(e1)
        for pair in range(2):
            ply_copy(e1 - 1, pair).wait_send()
        for f in (2, 3, 0, 1):
            if f in (2, 0):
                ply_copy(e1, f // 2).wait_recv()
            store_split(1, f, ply_rx[e1, f])
        acc[...] += product(shi, slo, 1)
        partial = jnp.zeros((8, cases), F32)
        for f in (0, 1, 2, 3):
            value = acc[pl.ds(f * face, face), :] + beta * sraw[f]
            sraw[f] = value
            face_send(e2, f, value)
            partial += jnp.sum((value * pdir[f]).reshape(face // 8, 8, cases), axis=0)
        reduce_first(k2, jnp.sum(partial, axis=0, keepdims=True))

        def assembled(f):
            face_wait(e2, f)
            own[e2, f] = sraw[f] + face_rx[e2, f]
            if f in (3, 1):

                @pl.when(it + 1 < ITERS)
                def _():
                    ply_copy(e2, f // 2).start()

        assembled(2)
        assembled(3)
        reduce_second(k2)
        assembled(0)
        assembled(1)
        for pair in range(2):
            ply_copy(e1, pair).wait_send()
        alpha = rz / reduce_end(k2)
        for f in range(4):
            part = pl.ds(f * face, face)
            x_ref[part, :] += alpha * pdir[f]
            r_ref[part, :] -= alpha * own[e2, f]
        reduce_sent(k2)
        faces_sent(e2)
        return -alpha

    lax.fori_loop(0, ITERS, iteration, jnp.ones((1, cases), F32))


def local(sizes, loads, schur, local_inverse, psi, face_map, primal_list, coarse_inverse):
    nb, nm, npl = sizes
    ng = nm * npl
    half, cases = loads.shape[2:]
    face = half // 4
    owned, coarse = coarse_inverse.shape
    group = ng * owned
    shape = jax.ShapeDtypeStruct((half, cases), F32)
    vmem = pl.BlockSpec(memory_space=pltpu.VMEM)
    smem = pl.BlockSpec(memory_space=pltpu.SMEM)
    hbm = pl.BlockSpec(memory_space=pl.ANY)
    faces = (4, face, cases)
    dma = pltpu.SemaphoreType.DMA
    scratch = (
        [pltpu.VMEM((2, half, half), F32)] * 2
        + [pltpu.VMEM((2, half, half), BF16)] * 4
        + [pltpu.VMEM((EXCH,) + faces, F32)] * 4
        + [pltpu.VMEM(faces, F32)] * 3
        + [
            pltpu.VMEM((half, cases), F32),
            pltpu.VMEM(faces, F32),
            pltpu.VMEM((2, half, 2 * cases), BF16),
            pltpu.VMEM((4, face, face), BF16),
            pltpu.VMEM((half, 3 * owned), BF16),
            pltpu.VMEM((2 * owned, half), BF16),
            pltpu.VMEM((5, owned, coarse), F32),
            pltpu.VMEM((nb + 2, owned, group), F32),
            pltpu.VMEM((nb, 3, owned, group), F32),
            pltpu.VMEM((nb * owned, group), F32),
            pltpu.VMEM((ng, owned, 128), jnp.int32),
            pltpu.VMEM((ITERS, ng, owned, cases), F32),
            pltpu.VMEM((ITERS, nb, owned, cases), F32),
            pltpu.VMEM((ITERS, nb, owned, cases), F32),
            pltpu.VMEM((2 * ITERS, ng, 1, cases), F32),
            pltpu.VMEM((2 * ITERS, nb, 1, cases), F32),
            pltpu.VMEM((1, cases), F32),
        ]
        + [dma((4,))]
        + [dma((EXCH, 4))] * 2
        + [dma((EXCH, 2))] * 2
        + [dma((4,))] * 2
        + [dma((1,))] * 4
        + [dma((ITERS,))] * 4
        + [dma((2 * ITERS,))] * 4
    )
    x, r = pl.pallas_call(
        functools.partial(kernel, sizes),
        out_shape=(shape, shape),
        in_specs=[vmem, hbm, hbm, vmem, vmem, smem, vmem],
        out_specs=(vmem, vmem),
        scratch_shapes=scratch,
        compiler_params=pltpu.CompilerParams(
            collective_id=0, has_side_effects=True, vmem_limit_bytes=56 * 1024 * 1024
        ),
        name="bddc_cg",
    )(
        loads[0, 0],
        schur[0, 0],
        local_inverse[0, 0],
        psi[0, 0],
        face_map[0, 0, 0],
        primal_list[0, 0, 0],
        coarse_inverse,
    )
    return x[None, None], r[None, None]


def solution(mesh):
    sizes = tuple(mesh.shape[axis] for axis in ("blk", "mer", "ply"))
    in_specs = (
        P("blk", "mer", "ply", None),
        P("blk", "mer", "ply", None),
        P("blk", "mer", "ply", None),
        P("blk", "mer", "ply", None),
        P("blk", "mer", "ply", None, None),
        P("blk", "mer", "ply", None),
        P(("blk", "mer", "ply"), None),
    )
    out_specs = (P("blk", "mer", "ply", None), P("blk", "mer", "ply", None))
    return jax.shard_map(
        functools.partial(local, sizes), mesh=mesh, in_specs=in_specs, out_specs=out_specs, check_vma=False
    )
```

```python
import functools

import jax
import jax.numpy as jnp
from jax import lax
from jax.experimental import pallas as pl
from jax.experimental.pallas import tpu as pltpu
from jax.sharding import PartitionSpec as P

ITERS = 4
EXCH = 2 * ITERS + 1
F32 = jnp.float32
BF16 = jnp.bfloat16
HIGH = lax.Precision.HIGHEST
MESH = pl.DeviceIdType.MESH
NT = (((1,), (1,)), ((), ()))


def halves(value):
    hi = value.astype(BF16)
    return hi, (value - hi.astype(F32)).astype(BF16)


def thirds(value):
    hi = value.astype(BF16)
    rest = value - hi.astype(F32)
    mid = rest.astype(BF16)
    return hi, mid, (rest - mid.astype(F32)).astype(BF16)


def dot(left, right):
    return jnp.dot(left, right, preferred_element_type=F32)


def remote(src, dst, send, recv, device):
    return pltpu.make_async_remote_copy(
        src_ref=src, dst_ref=dst, send_sem=send, recv_sem=recv, device_id=device, device_id_type=MESH
    )


def kernel(
    sizes,
    loads_ref, schur_ref, linv_ref, psi_ref, map_ref, list_ref, coarse_ref,
    x_ref, r_ref,
    lf, sf, lhi, llo, shi, slo,
    face_tx, face_rx, own, ply_rx,
    other, pdir, sraw, acc, gvec, tb, perm, psc, pst,
    fwd_tx, pmap, nbr, dpad, wblk, cblk, lists,
    co1, ytx, co2, ar1, ar2, rz_ref,
    load_sem, face_ss, face_rs, ply_ss, ply_rs, fwd_ss, map_ss, map_rs,
    nbr_ss, nbr_rs, win_ss, win_rs, list_ss, list_rs,
    co1_ss, co1_rs, co2_ss, co2_rs, ar1_ss, ar1_rs, ar2_ss, ar2_rs,
):
    nb, nm, npl = sizes
    ng = nm * npl
    half, cases = loads_ref.shape
    face = half // 4
    owned = coarse_ref.shape[0]
    b = lax.axis_index("blk")
    m = lax.axis_index("mer")
    p = lax.axis_index("ply")
    q = 1 - p
    mp = m * npl + p
    b_prev = lax.rem(b + nb - 1, nb)
    b_next = lax.rem(b + 1, nb)
    has_lo = m > 0
    has_hi = m < nm - 1
    weight = [
        0.5,
        0.5,
        jnp.where(has_lo, 0.5, 1.0).astype(F32),
        jnp.where(has_hi, 0.5, 1.0).astype(F32),
    ]
    partner = (b, m, q)
    neighbour = [(b_prev, m, p), (b_next, m, p), (b, m - 1, p), (b, m + 1, p)]
    exists = [None, None, has_lo, has_hi]
    run = nb // 2
    place = lax.rem(b, run)
    first = jnp.where(place < run // 2, 0, 1)
    second = 1 - first
    at_end = jnp.logical_or(place == 0, place == run - 1)
    serves_end = jnp.logical_or(place == 1, place == run - 2)
    toward_end = (jnp.where(first == 0, b_prev, b_next), m, p)

    def guarded(f, fn):
        if exists[f] is None:
            fn()
        else:
            pl.when(exists[f])(fn)

    def mp_device(index):
        return (b, lax.div(index, npl), lax.rem(index, npl))

    def blk_device(index):
        return (index, m, p)

    def spread(count, me, device_of, src_of, dst, send, recv):
        def step(j, carry):
            peer = lax.rem(me + j, count)
            remote(src_of(peer), dst, send, recv, device_of(peer)).start()
            return carry

        lax.fori_loop(1, count, step, 0)

    def fetch(index, source, side, target):
        column = pl.multiple_of(side * half, 128)
        return pltpu.make_async_copy(
            source.at[:, pl.ds(column, half)], target.at[index % 2], load_sem.at[index]
        )

    fetches = [
        fetch(0, linv_ref, p, lf),
        fetch(1, linv_ref, q, lf),
        fetch(2, schur_ref, p, sf),
        fetch(3, schur_ref, q, sf),
    ]
    for copy in fetches:
        copy.start()

    barrier = pltpu.get_barrier_semaphore()

    def greet(count, me, device_of):
        def step(j, carry):
            peer = lax.rem(me + j, count)
            pl.semaphore_signal(barrier, inc=1, device_id=device_of(peer), device_id_type=MESH)
            return carry

        lax.fori_loop(1, count, step, 0)

    greet(ng, mp, mp_device)
    greet(nb, b, blk_device)

    rows = lax.broadcasted_iota(jnp.int32, (face, face), 0)
    for f in range(4):
        perm[f] = jnp.where(rows == map_ref[f : f + 1, :], 1.0, 0.0).astype(BF16)

    for f in (2, 3):

        @pl.when(jnp.logical_not(exists[f]))
        def _():
            def clear(e, carry):
                face_rx[e, f] = jnp.zeros((face, cases), F32)
                return carry

            lax.fori_loop(0, EXCH, clear, 0)
            nbr[1 + f] = jnp.zeros(nbr.shape[1:], F32)

    map_copy = remote(map_ref, pmap, map_ss.at[0], map_rs.at[0], partner)

    lane = lax.broadcasted_iota(jnp.int32, (owned, lists.shape[2]), 1)
    sub = lax.broadcasted_iota(jnp.int32, (owned, lists.shape[2]), 0)
    mine = jnp.zeros_like(lane)
    for k in range(owned):
        mine = jnp.where(sub == k, list_ref[k], mine)
    lists[mp] = mine

    def permute(f, value):
        hi, mid, lo = thirds(value)
        out = dot(perm[f], jnp.concatenate([hi, mid, lo], axis=1))
        return (out[:, 2 * cases :] + out[:, cases : 2 * cases]) + out[:, :cases]

    def face_copy(e, f):
        return remote(
            face_tx.at[e, f], face_rx.at[e, f ^ 1], face_ss.at[e, f], face_rs.at[e, f ^ 1], neighbour[f]
        )

    def face_send(e, f, value):
        def go():
            face_tx[e, f] = permute(f, value)
            face_copy(e, f).start()

        guarded(f, go)

    def face_wait(e, f):
        guarded(
            f,
            lambda: remote(
                face_tx.at[e, f], face_rx.at[e, f], face_ss.at[e, f], face_rs.at[e, f], neighbour[f]
            ).wait_recv(),
        )

    def faces_sent(e):
        for f in range(4):
            guarded(f, lambda f=f: face_copy(e, f).wait_send())

    def ply_copy(e, f):
        return remote(own.at[e, f], ply_rx.at[e, f], ply_ss.at[e, f], ply_rs.at[e, f], partner)

    def mer_forward(e):
        return remote(
            fwd_tx.at[e, 0], ply_rx.at[e, 3], fwd_ss.at[e, 0], ply_rs.at[e, 3], neighbour[2]
        )

    def end_forward(e):
        return remote(
            fwd_tx.at[e, 1], ply_rx.at[e, second], fwd_ss.at[e, 1], ply_rs.at[e, second], toward_end
        )

    def when(condition, fn):
        pl.when(condition)(fn)

    def ply_send_mer(e):
        ply_copy(e, 2).start()
        when(jnp.logical_not(has_hi), lambda: ply_copy(e, 3).start())

    def ply_send_cycle(e):
        ply_copy(e, first).start()
        when(jnp.logical_not(at_end), lambda: ply_copy(e, second).start())

    def pass_mer(e):
        ply_copy(e, 2).wait_recv()

        @pl.when(has_lo)
        def _():
            fwd_tx[e, 0] = permute(6, ply_rx[e, 2])
            mer_forward(e).start()

    def pass_end(e):
        ply_copy(e, first).wait_recv()

        @pl.when(serves_end)
        def _():
            fwd_tx[e, 1] = permute(4 + first, ply_rx[e, first])
            end_forward(e).start()

    def ply_sent(e):
        ply_copy(e, 2).wait_send()
        when(jnp.logical_not(has_hi), lambda: ply_copy(e, 3).wait_send())
        ply_copy(e, first).wait_send()
        when(jnp.logical_not(at_end), lambda: ply_copy(e, second).wait_send())
        when(has_lo, lambda: mer_forward(e).wait_send())
        when(serves_end, lambda: end_forward(e).wait_send())

    def batch(buffer, index, count, send, recv):
        block = buffer.at[index, pl.ds(0, count - 1)]
        return remote(block, block, send, recv, partner)

    def reduce_first(k, value):
        ar1[k, mp] = value
        spread(ng, mp, mp_device, lambda _: ar1.at[k, mp], ar1.at[k, mp], ar1_ss.at[k], ar1_rs.at[k])

    def reduce_second(k):
        batch(ar1, k, ng, ar1_ss.at[k], ar1_rs.at[k]).wait_recv()
        ar2[k, b] = jnp.sum(ar1[k], axis=0)
        spread(nb, b, blk_device, lambda _: ar2.at[k, b], ar2.at[k, b], ar2_ss.at[k], ar2_rs.at[k])

    def reduce_end(k):
        batch(ar2, k, nb, ar2_ss.at[k], ar2_rs.at[k]).wait_recv()
        return jnp.sum(ar2[k], axis=0)

    def reduce_sent(k):
        batch(ar1, k, ng, ar1_ss.at[k], ar1_rs.at[k]).wait_send()
        batch(ar2, k, nb, ar2_ss.at[k], ar2_rs.at[k]).wait_send()

    def store_split(side, f, value):
        hi, lo = halves(value)
        part = pl.ds(f * face, face)
        tb[side, part, pl.ds(0, cases)] = hi
        tb[side, part, pl.ds(cases, cases)] = lo

    def product(hi, lo, side, pair):
        part = pl.ds(2 * pair * face, 2 * face)
        both = dot(hi[side, :, part], tb[side, part, :])
        small = dot(lo[side, :, part], tb[side, part, pl.ds(0, cases)])
        return (both[:, :cases] + both[:, cases:]) + small

    pl.semaphore_wait(barrier, ng - 1 + nb - 1)

    for f in (2, 3, 0, 1):
        face_send(0, f, loads_ref[pl.ds(f * face, face), :])

    slot_there = [2, 1, 4, 3]

    def nbr_copy(f):
        slot = slot_there[f]
        return remote(coarse_ref, nbr.at[slot], nbr_ss.at[f], nbr_rs.at[slot - 1], neighbour[f])

    for f in range(4):
        guarded(f, lambda f=f: nbr_copy(f).start())
    map_copy.start()
    nbr[0] = coarse_ref[...]
    spread(ng, mp, mp_device, lambda _: lists.at[mp], lists.at[mp], list_ss.at[0], list_rs.at[0])

    psi_hi, psi_lo = halves(psi_ref[...])
    psi_hi, psi_lo = psi_hi.astype(F32), psi_lo.astype(F32)
    pst[...] = jnp.concatenate([psi_hi, psi_lo], axis=0).astype(BF16)
    three = jnp.concatenate([psi_hi, psi_hi, psi_lo], axis=0).astype(BF16)
    eye_r = lax.broadcasted_iota(jnp.int32, (3 * owned, 3 * owned), 0)
    eye_c = lax.broadcasted_iota(jnp.int32, (3 * owned, 3 * owned), 1)
    eye = jnp.where(eye_r == eye_c, 1.0, 0.0).astype(BF16)
    psc[...] = lax.dot_general(
        three, eye, (((0,), (0,)), ((), ())), preferred_element_type=F32
    ).astype(BF16)

    def split_matrix(source, hi, lo):
        def step(i, carry):
            part = pl.ds(i * 64, 64)
            for side in range(2):
                a, c = halves(source[side, part, :])
                hi[side, part, :] = a
                lo[side, part, :] = c
            return carry

        lax.fori_loop(0, half // 64, step, 0)

    fetches[0].wait()
    fetches[1].wait()
    split_matrix(lf, lhi, llo)

    group = ng * owned
    this = (b * nm + m) * npl + p
    bases = [
        this * owned,
        ((b_prev * nm + m) * npl + p) * owned,
        ((b_next * nm + m) * npl + p) * owned,
        jnp.where(has_lo, (this - npl) * owned, -owned),
        jnp.where(has_hi, (this + npl) * owned, -owned),
    ]
    wide = lax.broadcasted_iota(jnp.int32, (owned, 5 * owned), 1)
    tall = lax.broadcasted_iota(jnp.int32, (owned, 5 * owned), 0)
    names = jnp.zeros_like(wide)
    for t in range(5):
        names = jnp.where(lax.div(wide, owned) == t, bases[t] + wide - t * owned, names)
    slots = jnp.zeros_like(wide)
    for k in range(owned):
        slots = jnp.where(tall == k, list_ref[k], slots)
    selector = jnp.where(slots == names, 1.0, 0.0).astype(F32)
    for f in range(4):
        guarded(
            f,
            lambda f=f: remote(
                coarse_ref, nbr.at[1 + f], nbr_ss.at[f], nbr_rs.at[f], neighbour[f]
            ).wait_recv(),
        )
    named = jnp.dot(
        selector, nbr[...].reshape(5 * owned, nbr.shape[2]), precision=HIGH, preferred_element_type=F32
    )
    for j in range(nb + 2):
        block = (j - 1) % nb
        dpad[j] = named[:, block * group : (block + 1) * group]
    wblk[b] = dpad[pl.ds(b, 3)]
    spread(nb, b, blk_device, lambda peer: dpad.at[pl.ds(peer, 3)], wblk.at[b], win_ss.at[0], win_rs.at[0])

    def first_residual(f):
        face_wait(0, f)
        value = loads_ref[pl.ds(f * face, face), :] + face_rx[0, f]
        own[0, f] = value
        r_ref[pl.ds(f * face, face), :] = value
        other[f] = jnp.zeros((face, cases), F32)

    first_residual(2)
    first_residual(3)
    ply_send_mer(0)
    first_residual(0)
    first_residual(1)
    ply_send_cycle(0)
    map_copy.wait_recv()
    for f in range(3):
        perm[4 + f] = jnp.where(rows == pmap[f : f + 1, :], 1.0, 0.0).astype(BF16)
    x_ref[...] = jnp.zeros_like(x_ref)
    pdir[...] = jnp.zeros_like(pdir)
    sraw[...] = jnp.zeros_like(sraw)
    rz_ref[...] = jnp.ones_like(rz_ref)

    block = lists.at[pl.ds(0, ng - 1)]
    remote(block, block, list_ss.at[0], list_rs.at[0], partner).wait_recv()
    names = lists[:, :, pl.ds(0, group)].reshape(group, group)
    column = lax.broadcasted_iota(jnp.int32, (group, group), 1)
    block = wblk.at[pl.ds(0, nb - 1)]
    remote(block, block, win_ss.at[0], win_rs.at[0], partner).wait_recv()
    total = jnp.zeros((nb * owned, group), F32)
    for j, start in enumerate((b_prev, b, b_next)):
        hot = jnp.where(names == column + start * group, 1.0, 0.0).astype(F32)
        window = wblk[:, j].reshape(nb * owned, group)
        total += lax.dot_general(window, hot, NT, precision=HIGH, preferred_element_type=F32)
    cblk[...] = total

    for f in range(4):
        guarded(f, lambda f=f: nbr_copy(f).wait_send())
    block = lists.at[pl.ds(0, ng - 1)]
    remote(block, block, list_ss.at[0], list_rs.at[0], partner).wait_send()
    block = wblk.at[pl.ds(0, nb - 1)]
    remote(block, block, win_ss.at[0], win_rs.at[0], partner).wait_send()
    map_copy.wait_send()
    faces_sent(0)

    def iteration(it, alpha):
        e1 = 1 + 2 * it
        e2 = 2 + 2 * it
        k1 = 2 * it
        k2 = 2 * it + 1

        for f in range(4):
            store_split(0, f, weight[f] * r_ref[pl.ds(f * face, face), :])
        parts = dot(pst[...], tb[0])
        terms = parts[:owned, :cases] + parts[:owned, cases:] + parts[owned:, :cases]
        co1[it, mp] = terms
        spread(ng, mp, mp_device, lambda _: co1.at[it, mp], co1.at[it, mp], co1_ss.at[it], co1_rs.at[it])
        pass_mer(e1 - 1)
        pass_end(e1 - 1)
        acc[...] = product(lhi, llo, 0, 1)
        acc[...] += product(lhi, llo, 0, 0)

        batch(co1, it, ng, co1_ss.at[it], co1_rs.at[it]).wait_recv()
        y = jnp.dot(
            cblk[...], co1[it].reshape(group, cases), precision=HIGH, preferred_element_type=F32
        )
        ytx[it] = y.reshape(nb, owned, cases)
        spread(nb, b, blk_device, lambda peer: ytx.at[it, peer], co2.at[it, b], co2_ss.at[it], co2_rs.at[it])
        co2[it, b] = ytx[it, b]

        @pl.when(it == 0)
        def _():
            fetches[2].wait()
            fetches[3].wait()
            split_matrix(sf, shi, slo)

        ply_copy(e1 - 1, 3).wait_recv()
        for pair in (1, 0):
            if pair == 0:
                ply_copy(e1 - 1, second).wait_recv()
            for f in (2 * pair, 2 * pair + 1):
                value = other[f] + alpha * ply_rx[e1 - 1, f]
                other[f] = value
                store_split(1, f, weight[f] * value)
            acc[...] += product(lhi, llo, 1, pair)

        batch(co2, it, nb, co2_ss.at[it], co2_rs.at[it]).wait_recv()
        picked = jnp.sum(co2[it], axis=0)
        pick_hi = picked.astype(BF16).astype(F32)
        stack = jnp.concatenate([pick_hi, picked - pick_hi, pick_hi], axis=0).astype(BF16)
        acc[...] += dot(psc[...], stack)

        partial = jnp.zeros((8, cases), F32)
        for f in (2, 3, 0, 1):
            part = pl.ds(f * face, face)
            value = weight[f] * acc[part, :]
            gvec[f] = value
            face_send(e1, f, value)
            partial += jnp.sum((value * r_ref[part, :]).reshape(face // 8, 8, cases), axis=0)
        reduce_first(k1, jnp.sum(partial, axis=0, keepdims=True))

        def assembled(f):
            face_wait(e1, f)
            value = gvec[f] + face_rx[e1, f]
            own[e1, f] = value
            store_split(0, f, value)

        assembled(2)
        assembled(3)
        ply_send_mer(e1)

        acc[...] = product(shi, slo, 0, 1)
        assembled(0)
        assembled(1)
        ply_send_cycle(e1)
        pass_mer(e1)
        reduce_second(k1)
        acc[...] += product(shi, slo, 0, 0)
        pass_end(e1)
        rz = reduce_end(k1)
        beta = jnp.where(it == 0, 0.0, rz / rz_ref[...])
        rz_ref[...] = rz
        for f in range(4):
            pdir[f] = own[e1, f] + beta * pdir[f]
        batch(co1, it, ng, co1_ss.at[it], co1_rs.at[it]).wait_send()
        batch(co2, it, nb, co2_ss.at[it], co2_rs.at[it]).wait_send()
        reduce_sent(k1)
        faces_sent(e1)
        ply_sent(e1 - 1)
        ply_copy(e1, 3).wait_recv()
        for pair in (1, 0):
            if pair == 0:
                ply_copy(e1, second).wait_recv()
            for f in (2 * pair, 2 * pair + 1):
                store_split(1, f, ply_rx[e1, f])
            acc[...] += product(shi, slo, 1, pair)
        partial = jnp.zeros((8, cases), F32)
        for f in range(4):
            value = acc[pl.ds(f * face, face), :] + beta * sraw[f]
            sraw[f] = value
            partial += jnp.sum((value * pdir[f]).reshape(face // 8, 8, cases), axis=0)
        reduce_first(k2, jnp.sum(partial, axis=0, keepdims=True))
        for f in (2, 3, 0, 1):
            face_send(e2, f, sraw[f])

        more = it + 1 < ITERS

        def image(f):
            face_wait(e2, f)
            own[e2, f] = sraw[f] + face_rx[e2, f]

        image(2)
        image(3)
        when(more, lambda: ply_send_mer(e2))
        reduce_second(k2)
        image(0)
        image(1)
        when(more, lambda: ply_send_cycle(e2))
        ply_sent(e1)
        alpha = rz / reduce_end(k2)
        for f in range(4):
            part = pl.ds(f * face, face)
            x_ref[part, :] += alpha * pdir[f]
            r_ref[part, :] -= alpha * own[e2, f]
        reduce_sent(k2)
        faces_sent(e2)
        return -alpha

    lax.fori_loop(0, ITERS, iteration, jnp.ones((1, cases), F32))


def deliver(x_ref, r_ref, x_out, r_out, sem):
    copies = [
        pltpu.make_async_copy(x_ref, x_out, sem.at[0]),
        pltpu.make_async_copy(r_ref, r_out, sem.at[1]),
    ]
    for copy in copies:
        copy.start()
    for copy in copies:
        copy.wait()


def local(sizes, loads, schur, local_inverse, psi, face_map, primal_list, coarse_inverse):
    nb, nm, npl = sizes
    ng = nm * npl
    half, cases = loads.shape[2:]
    face = half // 4
    owned, coarse = coarse_inverse.shape
    group = ng * owned
    shape = jax.ShapeDtypeStruct((half, cases), F32)
    vmem = pl.BlockSpec(memory_space=pltpu.VMEM)
    smem = pl.BlockSpec(memory_space=pltpu.SMEM)
    hbm = pl.BlockSpec(memory_space=pl.ANY)
    faces = (4, face, cases)
    dma = pltpu.SemaphoreType.DMA
    scratch = (
        [pltpu.VMEM((2, half, half), F32)] * 2
        + [pltpu.VMEM((2, half, half), BF16)] * 4
        + [pltpu.VMEM((EXCH,) + faces, F32)] * 4
        + [pltpu.VMEM(faces, F32)] * 3
        + [
            pltpu.VMEM((half, cases), F32),
            pltpu.VMEM(faces, F32),
            pltpu.VMEM((2, half, 2 * cases), BF16),
            pltpu.VMEM((7, face, face), BF16),
            pltpu.VMEM((half, 3 * owned), BF16),
            pltpu.VMEM((2 * owned, half), BF16),
            pltpu.VMEM((EXCH, 2, face, cases), F32),
            pltpu.VMEM((4, face), jnp.int32),
            pltpu.VMEM((5, owned, coarse), F32),
            pltpu.VMEM((nb + 2, owned, group), F32),
            pltpu.VMEM((nb, 3, owned, group), F32),
            pltpu.VMEM((nb * owned, group), F32),
            pltpu.VMEM((ng, owned, 128), jnp.int32),
            pltpu.VMEM((ITERS, ng, owned, cases), F32),
            pltpu.VMEM((ITERS, nb, owned, cases), F32),
            pltpu.VMEM((ITERS, nb, owned, cases), F32),
            pltpu.VMEM((2 * ITERS, ng, 1, cases), F32),
            pltpu.VMEM((2 * ITERS, nb, 1, cases), F32),
            pltpu.VMEM((1, cases), F32),
        ]
        + [dma((4,))]
        + [dma((EXCH, 4))] * 2
        + [dma((EXCH, 4))] * 2
        + [dma((EXCH, 2))]
        + [dma((1,))] * 2
        + [dma((4,))] * 2
        + [dma((1,))] * 4
        + [dma((ITERS,))] * 4
        + [dma((2 * ITERS,))] * 4
    )
    x, r = pl.pallas_call(
        functools.partial(kernel, sizes),
        out_shape=(shape, shape),
        in_specs=[vmem, hbm, hbm, vmem, vmem, smem, vmem],
        out_specs=(vmem, vmem),
        scratch_shapes=scratch,
        compiler_params=pltpu.CompilerParams(
            collective_id=0, has_side_effects=True, vmem_limit_bytes=56 * 1024 * 1024
        ),
        name="bddc_cg",
    )(
        loads[0, 0],
        schur[0, 0],
        local_inverse[0, 0],
        psi[0, 0].T,
        face_map[0, 0, 0],
        primal_list[0, 0, 0],
        coarse_inverse,
    )
    x, r = pl.pallas_call(
        deliver,
        out_shape=(shape, shape),
        in_specs=[hbm, hbm],
        out_specs=(hbm, hbm),
        scratch_shapes=[dma((2,))],
        name="deliver",
    )(x, r)
    return x[None, None], r[None, None]


def solution(mesh):
    sizes = tuple(mesh.shape[axis] for axis in ("blk", "mer", "ply"))
    in_specs = (
        P("blk", "mer", "ply", None),
        P("blk", "mer", "ply", None),
        P("blk", "mer", "ply", None),
        P("blk", "mer", "ply", None),
        P("blk", "mer", "ply", None, None),
        P("blk", "mer", "ply", None),
        P(("blk", "mer", "ply"), None),
    )
    out_specs = (P("blk", "mer", "ply", None), P("blk", "mer", "ply", None))
    return jax.shard_map(
        functools.partial(local, sizes), mesh=mesh, in_specs=in_specs, out_specs=out_specs, check_vma=False
    )
```

```python
import functools

import jax
import jax.numpy as jnp
from jax import lax
from jax.experimental import pallas as pl
from jax.experimental.pallas import tpu as pltpu
from jax.sharding import PartitionSpec as P

ITERS = 4
EXCH = 2 * ITERS + 1
F32 = jnp.float32
BF16 = jnp.bfloat16
HIGH = lax.Precision.HIGHEST
MESH = pl.DeviceIdType.MESH
NT = (((1,), (1,)), ((), ()))


def halves(value):
    hi = value.astype(BF16)
    return hi, (value - hi.astype(F32)).astype(BF16)


def thirds(value):
    hi = value.astype(BF16)
    rest = value - hi.astype(F32)
    mid = rest.astype(BF16)
    return hi, mid, (rest - mid.astype(F32)).astype(BF16)


def dot(left, right):
    return jnp.dot(left, right, preferred_element_type=F32)


def remote(src, dst, send, recv, device):
    return pltpu.make_async_remote_copy(
        src_ref=src, dst_ref=dst, send_sem=send, recv_sem=recv, device_id=device, device_id_type=MESH
    )


def kernel(
    sizes,
    loads_ref, schur_ref, linv_ref, psi_ref, map_ref, list_ref, coarse_ref,
    x_ref, r_ref,
    lf, sf, lhi, llo, shi, slo,
    face_tx, face_rx, own, ply_rx,
    pdir, simg, mdir, upre, raw, acc, tb, perm, psc, pst,
    fwd_tx, pmap, nbr, dpad, wblk, cblk, lists,
    sums, co1, ytx, co2, rz_ref, pap_ref,
    load_sem, face_ss, face_rs, ply_ss, ply_rs, fwd_ss, map_ss, map_rs,
    nbr_ss, nbr_rs, win_ss, win_rs, list_ss, list_rs,
    co1_ss, co1_rs, co2_ss, co2_rs,
):
    nb, nm, npl = sizes
    ng = nm * npl
    half, cases = loads_ref.shape
    face = half // 4
    owned = coarse_ref.shape[0]
    b = lax.axis_index("blk")
    m = lax.axis_index("mer")
    p = lax.axis_index("ply")
    q = 1 - p
    mp = m * npl + p
    b_prev = lax.rem(b + nb - 1, nb)
    b_next = lax.rem(b + 1, nb)
    has_lo = m > 0
    has_hi = m < nm - 1
    weight = [
        0.5,
        0.5,
        jnp.where(has_lo, 0.5, 1.0).astype(F32),
        jnp.where(has_hi, 0.5, 1.0).astype(F32),
    ]
    partner = (b, m, q)
    neighbour = [(b_prev, m, p), (b_next, m, p), (b, m - 1, p), (b, m + 1, p)]
    exists = [None, None, has_lo, has_hi]
    run = nb // 2
    place = lax.rem(b, run)
    first = jnp.where(place < run // 2, 0, 1)
    second = 1 - first
    at_end = jnp.logical_or(place == 0, place == run - 1)
    serves_end = jnp.logical_or(place == 1, place == run - 2)
    toward_end = (jnp.where(first == 0, b_prev, b_next), m, p)

    def guarded(f, fn):
        if exists[f] is None:
            fn()
        else:
            pl.when(exists[f])(fn)

    mp_devices = [(b, i // npl, i % npl) for i in range(ng)]
    blk_devices = [(i, m, p) for i in range(nb)]

    def spread(me, devices, src_of, dst, send, recv):
        for i, device in enumerate(devices):
            pl.when(me != i)(lambda: remote(src_of(i), dst, send, recv, device).start())

    def fetch(index, source, side, target):
        column = pl.multiple_of(side * half, 128)
        return pltpu.make_async_copy(
            source.at[:, pl.ds(column, half)], target.at[index % 2], load_sem.at[index]
        )

    fetches = [
        fetch(0, linv_ref, p, lf),
        fetch(1, linv_ref, q, lf),
        fetch(2, schur_ref, p, sf),
        fetch(3, schur_ref, q, sf),
    ]
    for copy in fetches:
        copy.start()

    barrier = pltpu.get_barrier_semaphore()

    def greet(me, devices):
        for i, device in enumerate(devices):

            @pl.when(me != i)
            def _():
                pl.semaphore_signal(barrier, inc=1, device_id=device, device_id_type=MESH)

    greet(mp, mp_devices)
    greet(b, blk_devices)

    rows = lax.broadcasted_iota(jnp.int32, (face, face), 0)
    for f in range(4):
        perm[f] = jnp.where(rows == map_ref[f : f + 1, :], 1.0, 0.0).astype(BF16)

    for f in (2, 3):

        @pl.when(jnp.logical_not(exists[f]))
        def _():
            def clear(e, carry):
                face_rx[e, f] = jnp.zeros((face, cases), F32)
                return carry

            lax.fori_loop(0, EXCH, clear, 0)
            nbr[1 + f] = jnp.zeros(nbr.shape[1:], F32)

    map_copy = remote(map_ref, pmap, map_ss.at[0], map_rs.at[0], partner)

    lane = lax.broadcasted_iota(jnp.int32, (owned, lists.shape[2]), 1)
    sub = lax.broadcasted_iota(jnp.int32, (owned, lists.shape[2]), 0)
    mine = jnp.zeros_like(lane)
    for k in range(owned):
        mine = jnp.where(sub == k, list_ref[k], mine)
    lists[mp] = mine

    def permute(f, value):
        hi, mid, lo = thirds(value)
        out = dot(perm[f], jnp.concatenate([hi, mid, lo], axis=1))
        return (out[:, 2 * cases :] + out[:, cases : 2 * cases]) + out[:, :cases]

    def face_copy(e, f):
        return remote(
            face_tx.at[e, f], face_rx.at[e, f ^ 1], face_ss.at[e, f], face_rs.at[e, f ^ 1], neighbour[f]
        )

    def face_send(e, f, value):
        def go():
            face_tx[e, f] = permute(f, value)
            face_copy(e, f).start()

        guarded(f, go)

    def face_wait(e, f):
        guarded(
            f,
            lambda: remote(
                face_tx.at[e, f], face_rx.at[e, f], face_ss.at[e, f], face_rs.at[e, f], neighbour[f]
            ).wait_recv(),
        )

    def faces_sent(e):
        for f in range(4):
            guarded(f, lambda f=f: face_copy(e, f).wait_send())

    def ply_copy(e, f):
        return remote(own.at[e, f], ply_rx.at[e, f], ply_ss.at[e, f], ply_rs.at[e, f], partner)

    def mer_forward(e):
        return remote(
            fwd_tx.at[e, 0], ply_rx.at[e, 3], fwd_ss.at[e, 0], ply_rs.at[e, 3], neighbour[2]
        )

    def end_forward(e):
        return remote(
            fwd_tx.at[e, 1], ply_rx.at[e, second], fwd_ss.at[e, 1], ply_rs.at[e, second], toward_end
        )

    def when(condition, fn):
        pl.when(condition)(fn)

    def ply_send_mer(e):
        ply_copy(e, 2).start()
        when(jnp.logical_not(has_hi), lambda: ply_copy(e, 3).start())

    def ply_send_cycle(e):
        ply_copy(e, first).start()
        when(jnp.logical_not(at_end), lambda: ply_copy(e, second).start())

    def pass_mer(e):
        ply_copy(e, 2).wait_recv()

        @pl.when(has_lo)
        def _():
            fwd_tx[e, 0] = permute(6, ply_rx[e, 2])
            mer_forward(e).start()

    def pass_end(e):
        ply_copy(e, first).wait_recv()

        @pl.when(serves_end)
        def _():
            fwd_tx[e, 1] = permute(4 + first, ply_rx[e, first])
            end_forward(e).start()

    def ply_sent(e):
        ply_copy(e, 2).wait_send()
        when(jnp.logical_not(has_hi), lambda: ply_copy(e, 3).wait_send())
        ply_copy(e, first).wait_send()
        when(jnp.logical_not(at_end), lambda: ply_copy(e, second).wait_send())
        when(has_lo, lambda: mer_forward(e).wait_send())
        when(serves_end, lambda: end_forward(e).wait_send())

    def batch(buffer, index, count, send, recv):
        block = buffer.at[index, pl.ds(0, count - 1)]
        return remote(block, block, send, recv, partner)

    def group_first(it, terms):
        co1[it, mp, pl.ds(0, owned)] = terms
        co1[it, mp, pl.ds(owned, 8)] = sums[...]
        spread(mp, mp_devices, lambda _: co1.at[it, mp], co1.at[it, mp], co1_ss.at[it], co1_rs.at[it])

    def group_second(it, coarse):
        batch(co1, it, ng, co1_ss.at[it], co1_rs.at[it]).wait_recv()
        if coarse:
            y = jnp.dot(
                cblk[...],
                co1[it, :, pl.ds(0, owned)].reshape(ng * owned, cases),
                precision=HIGH,
                preferred_element_type=F32,
            )
            ytx[it, :, pl.ds(0, owned)] = y.reshape(nb, owned, cases)
        else:
            ytx[it, :, pl.ds(0, owned)] = jnp.zeros((nb, owned, cases), F32)
        inner = jnp.sum(co1[it, :, pl.ds(owned, 8)], axis=0)
        ytx[it, :, pl.ds(owned, 8)] = jnp.broadcast_to(inner[None], (nb, 8, cases))
        spread(b, blk_devices, lambda i: ytx.at[it, i], co2.at[it, b], co2_ss.at[it], co2_rs.at[it])
        co2[it, b] = ytx[it, b]

    def group_end(it):
        batch(co2, it, nb, co2_ss.at[it], co2_rs.at[it]).wait_recv()
        total = jnp.sum(co2[it], axis=0)
        return total[:owned], total[owned : owned + 1], total[owned + 1 : owned + 2], total[owned + 2 : owned + 3]

    def group_sent(it):
        batch(co1, it, ng, co1_ss.at[it], co1_rs.at[it]).wait_send()
        batch(co2, it, nb, co2_ss.at[it], co2_rs.at[it]).wait_send()

    def rows_sum(value):
        return jnp.sum(value.reshape(face // 8, 8, cases), axis=0)

    def put_sums(parts):
        flat = [jnp.sum(part, axis=0, keepdims=True) for part in parts]
        index = lax.broadcasted_iota(jnp.int32, (8, cases), 0)
        out = jnp.zeros((8, cases), F32)
        for i, part in enumerate(flat):
            out = jnp.where(index == i, part, out)
        sums[...] = out

    def store_split(side, f, value):
        hi, lo = halves(value)
        part = pl.ds(f * face, face)
        tb[side, part, pl.ds(0, cases)] = hi
        tb[side, part, pl.ds(cases, cases)] = lo

    def product(hi, lo, side, pair):
        part = pl.ds(2 * pair * face, 2 * face)
        both = dot(hi[side, :, part], tb[side, part, :])
        small = dot(lo[side, :, part], tb[side, part, pl.ds(0, cases)])
        return (both[:, :cases] + both[:, cases:]) + small

    pl.semaphore_wait(barrier, ng - 1 + nb - 1)

    for f in (2, 3, 0, 1):
        raw[f] = loads_ref[pl.ds(f * face, face), :]
        face_send(0, f, raw[f])

    slot_there = [2, 1, 4, 3]

    def nbr_copy(f):
        slot = slot_there[f]
        return remote(coarse_ref, nbr.at[slot], nbr_ss.at[f], nbr_rs.at[slot - 1], neighbour[f])

    for f in range(4):
        guarded(f, lambda f=f: nbr_copy(f).start())
    map_copy.start()
    nbr[0] = coarse_ref[...]
    spread(mp, mp_devices, lambda _: lists.at[mp], lists.at[mp], list_ss.at[0], list_rs.at[0])

    psi_hi, psi_lo = halves(psi_ref[...])
    psi_hi, psi_lo = psi_hi.astype(F32), psi_lo.astype(F32)
    pst[...] = jnp.concatenate([psi_hi, psi_lo], axis=0).astype(BF16)
    three = jnp.concatenate([psi_hi, psi_hi, psi_lo], axis=0).astype(BF16)
    eye_r = lax.broadcasted_iota(jnp.int32, (3 * owned, 3 * owned), 0)
    eye_c = lax.broadcasted_iota(jnp.int32, (3 * owned, 3 * owned), 1)
    eye = jnp.where(eye_r == eye_c, 1.0, 0.0).astype(BF16)
    psc[...] = lax.dot_general(
        three, eye, (((0,), (0,)), ((), ())), preferred_element_type=F32
    ).astype(BF16)

    def split_matrix(source, hi, lo):
        def step(i, carry):
            part = pl.ds(i * 64, 64)
            for side in range(2):
                a, c = halves(source[side, part, :])
                hi[side, part, :] = a
                lo[side, part, :] = c
            return carry

        lax.fori_loop(0, half // 64, step, 0)

    fetches[0].wait()
    fetches[1].wait()
    split_matrix(lf, lhi, llo)

    group = ng * owned
    this = (b * nm + m) * npl + p
    bases = [
        this * owned,
        ((b_prev * nm + m) * npl + p) * owned,
        ((b_next * nm + m) * npl + p) * owned,
        jnp.where(has_lo, (this - npl) * owned, -owned),
        jnp.where(has_hi, (this + npl) * owned, -owned),
    ]
    wide = lax.broadcasted_iota(jnp.int32, (owned, 5 * owned), 1)
    tall = lax.broadcasted_iota(jnp.int32, (owned, 5 * owned), 0)
    names = jnp.zeros_like(wide)
    for t in range(5):
        names = jnp.where(lax.div(wide, owned) == t, bases[t] + wide - t * owned, names)
    slots = jnp.zeros_like(wide)
    for k in range(owned):
        slots = jnp.where(tall == k, list_ref[k], slots)
    selector = jnp.where(slots == names, 1.0, 0.0).astype(F32)
    for f in range(4):
        guarded(
            f,
            lambda f=f: remote(
                coarse_ref, nbr.at[1 + f], nbr_ss.at[f], nbr_rs.at[f], neighbour[f]
            ).wait_recv(),
        )
    named = jnp.dot(
        selector, nbr[...].reshape(5 * owned, nbr.shape[2]), precision=HIGH, preferred_element_type=F32
    )
    for j in range(nb + 2):
        block = (j - 1) % nb
        dpad[j] = named[:, block * group : (block + 1) * group]
    wblk[b] = dpad[pl.ds(b, 3)]
    spread(b, blk_devices, lambda peer: dpad.at[pl.ds(peer, 3)], wblk.at[b], win_ss.at[0], win_rs.at[0])

    map_copy.wait_recv()
    for f in range(3):
        perm[4 + f] = jnp.where(rows == pmap[f : f + 1, :], 1.0, 0.0).astype(BF16)
    for state in (x_ref, r_ref, pdir, simg, mdir, upre, pap_ref, sums):
        state[...] = jnp.zeros_like(state)
    rz_ref[...] = jnp.ones_like(rz_ref)

    def coarse_block():
        block = lists.at[pl.ds(0, ng - 1)]
        remote(block, block, list_ss.at[0], list_rs.at[0], partner).wait_recv()
        names = lists[:, :, pl.ds(0, group)].reshape(group, group)
        column = lax.broadcasted_iota(jnp.int32, (group, group), 1)
        block = wblk.at[pl.ds(0, nb - 1)]
        remote(block, block, win_ss.at[0], win_rs.at[0], partner).wait_recv()
        total = jnp.zeros((nb * owned, group), F32)
        for j, start in enumerate((b_prev, b, b_next)):
            hot = jnp.where(names == column + start * group, 1.0, 0.0).astype(F32)
            window = wblk[:, j].reshape(nb * owned, group)
            total += lax.dot_general(window, hot, NT, precision=HIGH, preferred_element_type=F32)
        cblk[...] = total
        for f in range(4):
            guarded(f, lambda f=f: nbr_copy(f).wait_send())
        block = lists.at[pl.ds(0, ng - 1)]
        remote(block, block, list_ss.at[0], list_rs.at[0], partner).wait_send()
        block = wblk.at[pl.ds(0, nb - 1)]
        remote(block, block, win_ss.at[0], win_rs.at[0], partner).wait_send()
        map_copy.wait_send()

    def assemble(e, pair, weights, ply):
        for f in (2 * pair, 2 * pair + 1):
            face_wait(e, f)
            value = raw[f] + face_rx[e, f]
            own[e, f] = value
        if ply and pair:
            ply_send_mer(e)
        elif ply:
            ply_send_cycle(e)
        if ply:
            for f in (2 * pair, 2 * pair + 1):
                value = own[e, f]
                store_split(0, f, value if weights is None else weights[f] * value)

    def exchange(e, hi, lo, weights, begin, middle):
        assemble(e, 1, weights, True)
        acc[...] = product(hi, lo, 0, 1)
        assemble(e, 0, weights, True)
        begin()
        pass_mer(e)
        acc[...] += product(hi, lo, 0, 0)
        pass_end(e)
        middle()
        ply_copy(e, 3).wait_recv()
        for pair in (1, 0):
            if pair == 0:
                ply_copy(e, second).wait_recv()
            for f in (2 * pair, 2 * pair + 1):
                value = ply_rx[e, f]
                store_split(1, f, value if weights is None else weights[f] * value)
            acc[...] += product(hi, lo, 1, pair)

    def steps(it, rz, energy, cross):
        beta = jnp.where(it <= 1, 0.0, rz / rz_ref[...])
        pap = (energy + 2.0 * beta * cross) + beta * beta * pap_ref[...]
        alpha = jnp.where(it == 0, -1.0, rz / pap)

        @pl.when(it > 0)
        def _():
            rz_ref[...] = rz
            pap_ref[...] = pap

        return alpha, beta

    def advance(e, alpha, beta):
        for f in range(4):
            part = pl.ds(f * face, face)
            value = own[e, f] + beta * simg[f]
            simg[f] = value
            r_ref[part, :] -= alpha * value

        @pl.when(e > 0)
        def _():
            for f in range(4):
                value = own[e - 1, f] + beta * pdir[f]
                pdir[f] = value
                x_ref[pl.ds(f * face, face), :] += alpha * value

    def iteration(it, carry):
        e1 = 2 * it
        e2 = e1 + 1

        def begin():
            parts = dot(pst[...], tb[0])
            group_first(it, parts[:owned, :cases] + parts[:owned, cases:] + parts[owned:, :cases])

        def middle():
            @pl.when(it == 0)
            def _():
                coarse_block()

            group_second(it, True)

            @pl.when(it == 0)
            def _():
                fetches[2].wait()
                fetches[3].wait()
                split_matrix(sf, shi, slo)

        exchange(e1, lhi, llo, weight, begin, middle)
        picked, rz, energy, cross = group_end(it)
        pick_hi = picked.astype(BF16).astype(F32)
        stack = jnp.concatenate([pick_hi, picked - pick_hi, pick_hi], axis=0).astype(BF16)
        acc[...] += dot(psc[...], stack)
        alpha, beta = steps(it, rz, energy, cross)
        for f in (2, 3, 0, 1):
            change = acc[pl.ds(f * face, face), :] + beta * mdir[f]
            mdir[f] = change
            value = upre[f] - alpha * change
            upre[f] = value
            value = weight[f] * value
            raw[f] = value
            face_send(e2, f, value)
        advance(e1, alpha, beta)
        partial = jnp.zeros((8, cases), F32)
        for f in range(4):
            partial += rows_sum(raw[f] * r_ref[pl.ds(f * face, face), :])
        faces_sent(e1)
        ply_sent(e1)
        group_sent(it)

        exchange(e2, shi, slo, None, lambda: None, lambda: None)
        for f in (2, 3, 0, 1):
            value = acc[pl.ds(f * face, face), :]
            raw[f] = value
            face_send(e2 + 1, f, value)
        energy = jnp.zeros((8, cases), F32)
        cross = jnp.zeros((8, cases), F32)
        for f in range(4):
            energy += rows_sum(raw[f] * own[e2, f])
            cross += rows_sum(raw[f] * pdir[f])
        put_sums((partial, energy, cross))
        faces_sent(e2)
        ply_sent(e2)
        return carry

    lax.fori_loop(0, ITERS, iteration, 0)

    last = EXCH - 1
    group_first(ITERS, jnp.zeros((owned, cases), F32))
    assemble(last, 1, None, False)
    group_second(ITERS, False)
    assemble(last, 0, None, False)
    _, rz, energy, cross = group_end(ITERS)
    alpha, beta = steps(ITERS, rz, energy, cross)
    advance(last, alpha, beta)
    faces_sent(last)
    group_sent(ITERS)


def deliver(x_ref, r_ref, x_out, r_out):
    x_out[...] = x_ref[...]
    r_out[...] = r_ref[...]


def local(sizes, loads, schur, local_inverse, psi, face_map, primal_list, coarse_inverse):
    nb, nm, npl = sizes
    ng = nm * npl
    half, cases = loads.shape[2:]
    face = half // 4
    owned, coarse = coarse_inverse.shape
    group = ng * owned
    shape = jax.ShapeDtypeStruct((half, cases), F32)
    vmem = pl.BlockSpec(memory_space=pltpu.VMEM)
    smem = pl.BlockSpec(memory_space=pltpu.SMEM)
    hbm = pl.BlockSpec(memory_space=pl.ANY)
    faces = (4, face, cases)
    dma = pltpu.SemaphoreType.DMA
    scratch = (
        [pltpu.VMEM((2, half, half), F32)] * 2
        + [pltpu.VMEM((2, half, half), BF16)] * 4
        + [pltpu.VMEM((EXCH,) + faces, F32)] * 4
        + [pltpu.VMEM(faces, F32)] * 5
        + [
            pltpu.VMEM((half, cases), F32),
            pltpu.VMEM((2, half, 2 * cases), BF16),
            pltpu.VMEM((7, face, face), BF16),
            pltpu.VMEM((half, 3 * owned), BF16),
            pltpu.VMEM((2 * owned, half), BF16),
            pltpu.VMEM((EXCH, 2, face, cases), F32),
            pltpu.VMEM((4, face), jnp.int32),
            pltpu.VMEM((5, owned, coarse), F32),
            pltpu.VMEM((nb + 2, owned, group), F32),
            pltpu.VMEM((nb, 3, owned, group), F32),
            pltpu.VMEM((nb * owned, group), F32),
            pltpu.VMEM((ng, owned, 128), jnp.int32),
            pltpu.VMEM((8, cases), F32),
            pltpu.VMEM((ITERS + 1, ng, owned + 8, cases), F32),
            pltpu.VMEM((ITERS + 1, nb, owned + 8, cases), F32),
            pltpu.VMEM((ITERS + 1, nb, owned + 8, cases), F32),
            pltpu.VMEM((1, cases), F32),
            pltpu.VMEM((1, cases), F32),
        ]
        + [dma((4,))]
        + [dma((EXCH, 4))] * 2
        + [dma((EXCH, 4))] * 2
        + [dma((EXCH, 2))]
        + [dma((1,))] * 2
        + [dma((4,))] * 2
        + [dma((1,))] * 4
        + [dma((ITERS + 1,))] * 4
    )
    x, r = pl.pallas_call(
        functools.partial(kernel, sizes),
        out_shape=(shape, shape),
        in_specs=[vmem, hbm, hbm, vmem, vmem, smem, vmem],
        out_specs=(vmem, vmem),
        scratch_shapes=scratch,
        compiler_params=pltpu.CompilerParams(
            collective_id=0, has_side_effects=True, vmem_limit_bytes=56 * 1024 * 1024
        ),
        name="bddc_cg",
    )(
        loads[0, 0],
        schur[0, 0],
        local_inverse[0, 0],
        psi[0, 0].T,
        face_map[0, 0, 0],
        primal_list[0, 0, 0],
        coarse_inverse,
    )
    x, r = pl.pallas_call(
        deliver,
        out_shape=(shape, shape),
        in_specs=[vmem, vmem],
        out_specs=(vmem, vmem),
        name="deliver",
    )(x, r)
    return x[None, None], r[None, None]


def solution(mesh):
    sizes = tuple(mesh.shape[axis] for axis in ("blk", "mer", "ply"))
    in_specs = (
        P("blk", "mer", "ply", None),
        P("blk", "mer", "ply", None),
        P("blk", "mer", "ply", None),
        P("blk", "mer", "ply", None),
        P("blk", "mer", "ply", None, None),
        P("blk", "mer", "ply", None),
        P(("blk", "mer", "ply"), None),
    )
    out_specs = (P("blk", "mer", "ply", None), P("blk", "mer", "ply", None))
    return jax.shard_map(
        functools.partial(local, sizes), mesh=mesh, in_specs=in_specs, out_specs=out_specs, check_vma=False
    )
```

```python
import functools

import jax
import jax.numpy as jnp
from jax import lax
from jax.experimental import pallas as pl
from jax.experimental.pallas import tpu as pltpu
from jax.sharding import PartitionSpec as P

ITERS = 4
EXCH = 2 * ITERS + 1
F32 = jnp.float32
BF16 = jnp.bfloat16
HIGH = lax.Precision.HIGHEST
MESH = pl.DeviceIdType.MESH
NT = (((1,), (1,)), ((), ()))


def halves(value):
    hi = value.astype(BF16)
    return hi, (value - hi.astype(F32)).astype(BF16)


def thirds(value):
    hi = value.astype(BF16)
    rest = value - hi.astype(F32)
    mid = rest.astype(BF16)
    return hi, mid, (rest - mid.astype(F32)).astype(BF16)


def dot(left, right):
    return jnp.dot(left, right, preferred_element_type=F32)


def remote(src, dst, send, recv, device):
    return pltpu.make_async_remote_copy(
        src_ref=src, dst_ref=dst, send_sem=send, recv_sem=recv, device_id=device, device_id_type=MESH
    )


def kernel(
    sizes,
    loads_ref, schur_ref, linv_ref, psi_ref, map_ref, list_ref, coarse_ref,
    x_ref, r_ref,
    lf, sf, lhi, llo, shi, slo,
    face_tx, face_rx, own, ply_rx,
    pdir, simg, mdir, upre, raw, acc, tb, perm, psc, pst,
    fwd_tx, pmap, nbr, dpad, wblk, chi, clo, lists, psn_tx, psn_rx, psn, tsm_tx, tsm_rx,
    sums, co1, ytx, co2, rz_ref, pap_ref,
    load_sem, face_ss, face_rs, ply_ss, ply_rs, fwd_ss, map_ss, map_rs,
    nbr_ss, nbr_rs, win_ss, win_rs, list_ss, list_rs,
    co1_ss, co1_rs, co2_ss, co2_rs, psn_ss, psn_rs, tsm_ss, tsm_rs,
):
    nb, nm, npl = sizes
    ng = nm * npl
    half, cases = loads_ref.shape
    face = half // 4
    owned = coarse_ref.shape[0]
    b = lax.axis_index("blk")
    m = lax.axis_index("mer")
    p = lax.axis_index("ply")
    q = 1 - p
    mp = m * npl + p
    b_prev = lax.rem(b + nb - 1, nb)
    b_next = lax.rem(b + 1, nb)
    has_lo = m > 0
    has_hi = m < nm - 1
    weight = [
        0.5,
        0.5,
        jnp.where(has_lo, 0.5, 1.0).astype(F32),
        jnp.where(has_hi, 0.5, 1.0).astype(F32),
    ]
    partner = (b, m, q)
    neighbour = [(b_prev, m, p), (b_next, m, p), (b, m - 1, p), (b, m + 1, p)]
    exists = [None, None, has_lo, has_hi]
    run = nb // 2
    place = lax.rem(b, run)
    first = jnp.where(place < run // 2, 0, 1)
    second = 1 - first
    at_end = jnp.logical_or(place == 0, place == run - 1)
    serves_end = jnp.logical_or(place == 1, place == run - 2)
    toward_end = (jnp.where(first == 0, b_prev, b_next), m, p)
    from_end = (jnp.where(first == 0, b_next, b_prev), m, p)

    def device_at(f):
        if isinstance(f, int):
            return neighbour[f]
        return toward_end if f is first else from_end

    def opposite(f):
        return f ^ 1 if isinstance(f, int) else 1 - f

    def weight_of(f):
        return weight[f] if isinstance(f, int) else 0.5

    def guarded(f, fn):
        if not isinstance(f, int) or exists[f] is None:
            fn()
        else:
            pl.when(exists[f])(fn)

    mp_devices = [(b, i // npl, i % npl) for i in range(ng)]
    blk_devices = [(i, m, p) for i in range(nb)]

    def spread(me, devices, src_of, dst, send, recv):
        for i, device in enumerate(devices):
            pl.when(me != i)(lambda: remote(src_of(i), dst, send, recv, device).start())

    def fetch(index, source, side, target):
        column = pl.multiple_of(side * half, 128)
        return pltpu.make_async_copy(
            source.at[:, pl.ds(column, half)], target.at[index % 2], load_sem.at[index]
        )

    fetches = [
        fetch(0, linv_ref, p, lf),
        fetch(1, linv_ref, q, lf),
        fetch(2, schur_ref, p, sf),
        fetch(3, schur_ref, q, sf),
    ]
    for copy in fetches:
        copy.start()

    barrier = pltpu.get_barrier_semaphore()

    def greet(me, devices):
        for i, device in enumerate(devices):

            @pl.when(me != i)
            def _():
                pl.semaphore_signal(barrier, inc=1, device_id=device, device_id_type=MESH)

    greet(mp, mp_devices)
    greet(b, blk_devices)

    rows = lax.broadcasted_iota(jnp.int32, (face, face), 0)
    for f in range(4):
        perm[f] = jnp.where(rows == map_ref[f : f + 1, :], 1.0, 0.0).astype(BF16)

    for f in (2, 3):

        @pl.when(jnp.logical_not(exists[f]))
        def _():
            def clear(e, carry):
                face_rx[e, f] = jnp.zeros((face, cases), F32)
                return carry

            lax.fori_loop(0, EXCH, clear, 0)
            nbr[1 + f] = jnp.zeros(nbr.shape[1:], F32)
            for it in range(ITERS):
                tsm_rx[it, f] = jnp.zeros((owned, cases), F32)

    map_copy = remote(map_ref, pmap, map_ss.at[0], map_rs.at[0], partner)

    lane = lax.broadcasted_iota(jnp.int32, (owned, lists.shape[2]), 1)
    sub = lax.broadcasted_iota(jnp.int32, (owned, lists.shape[2]), 0)
    mine = jnp.zeros_like(lane)
    for k in range(owned):
        mine = jnp.where(sub == k, list_ref[k], mine)
    lists[mp] = mine

    def permute(f, value):
        hi, mid, lo = thirds(value)
        out = dot(perm[f], jnp.concatenate([hi, mid, lo], axis=1))
        return (out[:, 2 * cases :] + out[:, cases : 2 * cases]) + out[:, :cases]

    def face_copy(e, f):
        there = opposite(f)
        return remote(
            face_tx.at[e, f], face_rx.at[e, there], face_ss.at[e, f], face_rs.at[e, there], device_at(f)
        )

    def face_send(e, f):
        def go():
            face_tx[e, f] = permute(f, raw[f])
            face_copy(e, f).start()

        guarded(f, go)

    def faces_send(e):
        pl.when(at_end)(lambda: face_send(e, first))
        face_send(e, 2)
        face_send(e, 3)
        pl.when(jnp.logical_not(at_end))(lambda: face_send(e, first))
        face_send(e, second)

    def face_wait(e, f):
        guarded(
            f,
            lambda: remote(
                face_tx.at[e, f], face_rx.at[e, f], face_ss.at[e, f], face_rs.at[e, f], device_at(f)
            ).wait_recv(),
        )

    def faces_sent(e):
        for f in range(4):
            guarded(f, lambda f=f: face_copy(e, f).wait_send())

    def ply_copy(e, f):
        return remote(own.at[e, f], ply_rx.at[e, f], ply_ss.at[e, f], ply_rs.at[e, f], partner)

    def mer_forward(e):
        return remote(
            fwd_tx.at[e, 0], ply_rx.at[e, 3], fwd_ss.at[e, 0], ply_rs.at[e, 3], neighbour[2]
        )

    def end_forward(e):
        return remote(
            fwd_tx.at[e, 1], ply_rx.at[e, second], fwd_ss.at[e, 1], ply_rs.at[e, second], toward_end
        )

    def when(condition, fn):
        pl.when(condition)(fn)

    def ply_send_mer(e):
        ply_copy(e, 2).start()
        when(jnp.logical_not(has_hi), lambda: ply_copy(e, 3).start())

    def pass_mer(e):
        ply_copy(e, 2).wait_recv()

        @pl.when(has_lo)
        def _():
            fwd_tx[e, 0] = permute(6, ply_rx[e, 2])
            mer_forward(e).start()

    def pass_end(e):
        ply_copy(e, first).wait_recv()

        @pl.when(serves_end)
        def _():
            fwd_tx[e, 1] = permute(4 + first, ply_rx[e, first])
            end_forward(e).start()

    def ply_sent(e):
        ply_copy(e, 2).wait_send()
        when(jnp.logical_not(has_hi), lambda: ply_copy(e, 3).wait_send())
        ply_copy(e, first).wait_send()
        when(jnp.logical_not(at_end), lambda: ply_copy(e, second).wait_send())
        when(has_lo, lambda: mer_forward(e).wait_send())
        when(serves_end, lambda: end_forward(e).wait_send())

    def batch(buffer, index, count, send, recv):
        block = buffer.at[index, pl.ds(0, count - 1)]
        return remote(block, block, send, recv, partner)

    def group_first(it, terms):
        co1[it, mp, pl.ds(0, owned)] = terms
        co1[it, mp, pl.ds(owned, 8)] = sums[...]
        spread(mp, mp_devices, lambda _: co1.at[it, mp], co1.at[it, mp], co1_ss.at[it], co1_rs.at[it])

    def group_second(it, coarse):
        batch(co1, it, ng, co1_ss.at[it], co1_rs.at[it]).wait_recv()
        if coarse:
            high, low = halves(co1[it, :, pl.ds(0, owned)].reshape(ng * owned, cases))
            both = dot(chi[...], jnp.concatenate([high, low], axis=1))
            y = (both[:, :cases] + both[:, cases:]) + dot(clo[...], high)
            ytx[it, :, pl.ds(0, owned)] = y.reshape(nb, owned, cases)
        else:
            ytx[it, :, pl.ds(0, owned)] = jnp.zeros((nb, owned, cases), F32)
        inner = jnp.sum(co1[it, :, pl.ds(owned, 8)], axis=0)
        ytx[it, :, pl.ds(owned, 8)] = jnp.broadcast_to(inner[None], (nb, 8, cases))
        spread(b, blk_devices, lambda i: ytx.at[it, i], co2.at[it, b], co2_ss.at[it], co2_rs.at[it])
        co2[it, b] = ytx[it, b]

    def group_end(it):
        batch(co2, it, nb, co2_ss.at[it], co2_rs.at[it]).wait_recv()
        total = jnp.sum(co2[it], axis=0)
        return total[:owned], total[owned : owned + 1], total[owned + 1 : owned + 2], total[owned + 2 : owned + 3]

    def group_sent(it):
        batch(co1, it, ng, co1_ss.at[it], co1_rs.at[it]).wait_send()
        batch(co2, it, nb, co2_ss.at[it], co2_rs.at[it]).wait_send()

    def rows_sum(value):
        return jnp.sum(value.reshape(face // 8, 8, cases), axis=0)

    def put_sums(parts):
        flat = [jnp.sum(part, axis=0, keepdims=True) for part in parts]
        index = lax.broadcasted_iota(jnp.int32, (8, cases), 0)
        out = jnp.zeros((8, cases), F32)
        for i, part in enumerate(flat):
            out = jnp.where(index == i, part, out)
        sums[...] = out

    def store_split(side, f, value):
        hi, lo = halves(value)
        tb[side, f, :, pl.ds(0, cases)] = hi
        tb[side, f, :, pl.ds(cases, cases)] = lo

    def product(hi, lo, side, pair):
        part = pl.ds(2 * pair * face, 2 * face)
        vector = tb[side, pl.ds(2 * pair, 2)].reshape(2 * face, 2 * cases)
        both = dot(hi[side, :, part], vector)
        small = dot(lo[side, :, part], vector[:, :cases])
        return ((both[:, :cases] + both[:, cases:]) + small).reshape(4, face, cases)

    def terms_copy(it, f):
        there = opposite(f)
        return remote(
            tsm_tx.at[it, f], tsm_rx.at[it, there], tsm_ss.at[it, f], tsm_rs.at[it, there], device_at(f)
        )

    def three_parts(value):
        return value[:owned, :cases] + value[:owned, cases:] + value[owned:, :cases]

    def terms_send(it):
        for f in range(4):
            store_split(1, f, weight[f] * raw[f])
        for f in (0, 1, 2, 3):

            def go():
                tsm_tx[it, f] = three_parts(dot(psn[f], tb[1, f]))
                terms_copy(it, f).start()

            guarded(f, go)
        co1[it, mp, pl.ds(0, owned)] = three_parts(dot(pst[...], tb[1].reshape(half, 2 * cases)))

    def terms_end(it):
        total = co1[it, mp, pl.ds(0, owned)]
        for f in (2, 3, 0, 1):
            guarded(
                f,
                lambda: remote(
                    tsm_tx.at[it, f], tsm_rx.at[it, f], tsm_ss.at[it, f], tsm_rs.at[it, f], device_at(f)
                ).wait_recv(),
            )
            total += tsm_rx[it, f]
        return total

    def terms_sent(it):
        for f in range(4):
            guarded(f, lambda f=f: terms_copy(it, f).wait_send())

    pl.semaphore_wait(barrier, ng - 1 + nb - 1)

    def psn_copy(f):
        there = opposite(f)
        return remote(psn_tx.at[f], psn_rx.at[there], psn_ss.at[f], psn_rs.at[there], device_at(f))

    for f in range(4):

        def go():
            hi, mid, lo = thirds(psi_ref[:, pl.ds(f * face, face)])
            stacked = jnp.concatenate(
                [hi.astype(F32), mid.astype(F32), lo.astype(F32)], axis=0
            ).astype(BF16)
            out = lax.dot_general(stacked, perm[f], NT, preferred_element_type=F32)
            psn_tx[f] = (out[2 * owned :] + out[owned : 2 * owned]) + out[:owned]
            psn_copy(f).start()

        guarded(f, go)

    slot_there = [2, 1, 4, 3]

    def nbr_copy(f):
        slot = slot_there[f]
        return remote(coarse_ref, nbr.at[slot], nbr_ss.at[f], nbr_rs.at[slot - 1], neighbour[f])

    for f in range(4):
        guarded(f, lambda f=f: nbr_copy(f).start())
    map_copy.start()
    nbr[0] = coarse_ref[...]
    spread(mp, mp_devices, lambda _: lists.at[mp], lists.at[mp], list_ss.at[0], list_rs.at[0])

    for f in range(4):
        raw[f] = loads_ref[pl.ds(f * face, face), :]
    faces_send(0)

    psi_hi, psi_lo = halves(psi_ref[...])
    psi_hi, psi_lo = psi_hi.astype(F32), psi_lo.astype(F32)
    pst[...] = jnp.concatenate([psi_hi, psi_lo], axis=0).astype(BF16)
    three = jnp.concatenate([psi_hi, psi_hi, psi_lo], axis=0).astype(BF16)
    eye_r = lax.broadcasted_iota(jnp.int32, (3 * owned, 3 * owned), 0)
    eye_c = lax.broadcasted_iota(jnp.int32, (3 * owned, 3 * owned), 1)
    eye = jnp.where(eye_r == eye_c, 1.0, 0.0).astype(BF16)
    psc[...] = lax.dot_general(
        three, eye, (((0,), (0,)), ((), ())), preferred_element_type=F32
    ).astype(BF16)

    def split_matrix(source, hi, lo):
        def step(i, carry):
            part = pl.ds(i * 64, 64)
            for side in range(2):
                a, c = halves(source[side, part, :])
                hi[side, part, :] = a
                lo[side, part, :] = c
            return carry

        lax.fori_loop(0, half // 64, step, 0)

    for f in range(4):

        def go():
            remote(
                psn_tx.at[f], psn_rx.at[f], psn_ss.at[f], psn_rs.at[f], device_at(f)
            ).wait_recv()
            hi, lo = halves(psn_rx[f])
            psn[f] = jnp.concatenate([hi.astype(F32), lo.astype(F32)], axis=0).astype(BF16)

        guarded(f, go)
    terms_send(0)

    group = ng * owned
    this = (b * nm + m) * npl + p
    bases = [
        this * owned,
        ((b_prev * nm + m) * npl + p) * owned,
        ((b_next * nm + m) * npl + p) * owned,
        jnp.where(has_lo, (this - npl) * owned, -owned),
        jnp.where(has_hi, (this + npl) * owned, -owned),
    ]
    wide = lax.broadcasted_iota(jnp.int32, (owned, 5 * owned), 1)
    tall = lax.broadcasted_iota(jnp.int32, (owned, 5 * owned), 0)
    names = jnp.zeros_like(wide)
    for t in range(5):
        names = jnp.where(lax.div(wide, owned) == t, bases[t] + wide - t * owned, names)
    slots = jnp.zeros_like(wide)
    for k in range(owned):
        slots = jnp.where(tall == k, list_ref[k], slots)
    selector = jnp.where(slots == names, 1.0, 0.0).astype(F32)
    for f in range(4):
        guarded(
            f,
            lambda f=f: remote(
                coarse_ref, nbr.at[1 + f], nbr_ss.at[f], nbr_rs.at[f], neighbour[f]
            ).wait_recv(),
        )
    hot = selector.astype(BF16)
    hi, mid, lo = thirds(nbr[...].reshape(5 * owned, nbr.shape[2]))
    named = (dot(hot, lo) + dot(hot, mid)) + dot(hot, hi)
    for j in range(nb + 2):
        block = (j - 1) % nb
        dpad[j] = named[:, block * group : (block + 1) * group]
    wblk[b] = dpad[pl.ds(b, 3)]
    spread(b, blk_devices, lambda peer: dpad.at[pl.ds(peer, 3)], wblk.at[b], win_ss.at[0], win_rs.at[0])

    fetches[0].wait()
    fetches[1].wait()
    split_matrix(lf, lhi, llo)
    map_copy.wait_recv()
    for f in range(3):
        perm[4 + f] = jnp.where(rows == pmap[f : f + 1, :], 1.0, 0.0).astype(BF16)
    for state in (x_ref, r_ref, pdir, simg, mdir, upre, pap_ref, sums):
        state[...] = jnp.zeros_like(state)
    rz_ref[...] = jnp.ones_like(rz_ref)

    def coarse_block():
        block = lists.at[pl.ds(0, ng - 1)]
        remote(block, block, list_ss.at[0], list_rs.at[0], partner).wait_recv()
        names = lists[:, :, pl.ds(0, group)].reshape(group, group)
        column = lax.broadcasted_iota(jnp.int32, (group, group), 1)
        block = wblk.at[pl.ds(0, nb - 1)]
        remote(block, block, win_ss.at[0], win_rs.at[0], partner).wait_recv()
        total = jnp.zeros((nb * owned, group), F32)
        for j, start in enumerate((b_prev, b, b_next)):
            hot = jnp.where(names == column + start * group, 1.0, 0.0).astype(BF16)
            window = wblk[:, j].reshape(nb * owned, group)
            hi, mid, lo = (
                lax.dot_general(piece, hot, NT, preferred_element_type=F32) for piece in thirds(window)
            )
            total += (lo + mid) + hi
        chi[...], clo[...] = halves(total)
        for f in range(4):
            guarded(f, lambda f=f: psn_copy(f).wait_send())
        for f in range(4):
            guarded(f, lambda f=f: nbr_copy(f).wait_send())
        block = lists.at[pl.ds(0, ng - 1)]
        remote(block, block, list_ss.at[0], list_rs.at[0], partner).wait_send()
        block = wblk.at[pl.ds(0, nb - 1)]
        remote(block, block, win_ss.at[0], win_rs.at[0], partner).wait_send()
        map_copy.wait_send()

    def assemble(e, f):
        face_wait(e, f)
        own[e, f] = raw[f] + face_rx[e, f]

    def exchange(e, hi, lo, weights, early, middle):
        def scaled(f, value):
            return value if weights is None else weight_of(f) * value

        def take(f):
            assemble(e, f)
            store_split(0, f, scaled(f, own[e, f]))

        def add(side, pair):
            acc[...] += product(hi, lo, side, pair)

        take(2)
        take(3)
        ply_send_mer(e)
        early()
        acc[...] = product(hi, lo, 0, 1)
        take(second)

        @pl.when(jnp.logical_not(at_end))
        def _():
            take(first)
            ply_copy(e, first).start()
            ply_copy(e, second).start()
            add(0, 0)

        pass_mer(e)
        middle()

        @pl.when(at_end)
        def _():
            take(first)
            ply_copy(e, first).start()
            add(0, 0)

        pass_end(e)
        ply_copy(e, 3).wait_recv()
        for pair in (1, 0):
            if pair == 0:
                ply_copy(e, second).wait_recv()
            for f in (2 * pair, 2 * pair + 1):
                store_split(1, f, scaled(f, ply_rx[e, f]))
            add(1, pair)

    def steps(it, rz, energy, cross):
        beta = jnp.where(it <= 1, 0.0, rz / rz_ref[...])
        pap = (energy + 2.0 * beta * cross) + beta * beta * pap_ref[...]
        alpha = jnp.where(it == 0, -1.0, rz / pap)

        @pl.when(it > 0)
        def _():
            rz_ref[...] = rz
            pap_ref[...] = pap

        return alpha, beta

    def advance(e, alpha, beta):
        for f in range(4):
            part = pl.ds(f * face, face)
            value = own[e, f] + beta * simg[f]
            simg[f] = value
            r_ref[part, :] -= alpha * value

        @pl.when(e > 0)
        def _():
            for f in range(4):
                value = own[e - 1, f] + beta * pdir[f]
                pdir[f] = value
                x_ref[pl.ds(f * face, face), :] += alpha * value

    def iteration(it, carry):
        e1 = 2 * it
        e2 = e1 + 1

        def early():
            group_first(it, terms_end(it))

        def middle():
            @pl.when(it == 0)
            def _():
                coarse_block()

            group_second(it, True)

            @pl.when(it == 0)
            def _():
                fetches[2].wait()
                fetches[3].wait()
                split_matrix(sf, shi, slo)

        exchange(e1, lhi, llo, weight, early, middle)
        picked, rz, energy, cross = group_end(it)
        pick_hi = picked.astype(BF16).astype(F32)
        stack = jnp.concatenate([pick_hi, picked - pick_hi, pick_hi], axis=0).astype(BF16)
        correction = dot(psc[...], stack).reshape(4, face, cases)
        alpha, beta = steps(it, rz, energy, cross)
        for f in range(4):
            change = (acc[f] + correction[f]) + beta * mdir[f]
            mdir[f] = change
            value = upre[f] - alpha * change
            upre[f] = value
            raw[f] = weight[f] * value
        faces_send(e2)
        advance(e1, alpha, beta)
        partial = jnp.zeros((8, cases), F32)
        for f in range(4):
            partial += rows_sum(raw[f] * r_ref[pl.ds(f * face, face), :])
        faces_sent(e1)
        ply_sent(e1)
        group_sent(it)
        terms_sent(it)

        exchange(e2, shi, slo, None, lambda: None, lambda: None)
        raw[...] = acc[...]
        pl.when(it + 1 < ITERS)(lambda: terms_send(it + 1))
        faces_send(e2 + 1)
        energy = jnp.zeros((8, cases), F32)
        cross = jnp.zeros((8, cases), F32)
        for f in range(4):
            energy += rows_sum(raw[f] * own[e2, f])
            cross += rows_sum(raw[f] * pdir[f])
        put_sums((partial, energy, cross))
        faces_sent(e2)
        ply_sent(e2)
        return carry

    lax.fori_loop(0, ITERS, iteration, 0)

    last = EXCH - 1
    group_first(ITERS, jnp.zeros((owned, cases), F32))
    assemble(last, 2)
    assemble(last, 3)
    group_second(ITERS, False)
    assemble(last, 0)
    assemble(last, 1)
    _, rz, energy, cross = group_end(ITERS)
    alpha, beta = steps(ITERS, rz, energy, cross)
    advance(last, alpha, beta)
    faces_sent(last)
    group_sent(ITERS)


def deliver(x_ref, r_ref, x_out, r_out):
    x_out[...] = x_ref[...]
    r_out[...] = r_ref[...]


def local(sizes, loads, schur, local_inverse, psi, face_map, primal_list, coarse_inverse):
    nb, nm, npl = sizes
    ng = nm * npl
    half, cases = loads.shape[2:]
    face = half // 4
    owned, coarse = coarse_inverse.shape
    group = ng * owned
    shape = jax.ShapeDtypeStruct((half, cases), F32)
    vmem = pl.BlockSpec(memory_space=pltpu.VMEM)
    smem = pl.BlockSpec(memory_space=pltpu.SMEM)
    hbm = pl.BlockSpec(memory_space=pl.ANY)
    faces = (4, face, cases)
    dma = pltpu.SemaphoreType.DMA
    scratch = (
        [pltpu.VMEM((2, half, half), F32)] * 2
        + [pltpu.VMEM((2, half, half), BF16)] * 4
        + [pltpu.VMEM((EXCH,) + faces, F32)] * 4
        + [pltpu.VMEM(faces, F32)] * 5
        + [
            pltpu.VMEM(faces, F32),
            pltpu.VMEM((2, 4, face, 2 * cases), BF16),
            pltpu.VMEM((7, face, face), BF16),
            pltpu.VMEM((half, 3 * owned), BF16),
            pltpu.VMEM((2 * owned, half), BF16),
            pltpu.VMEM((EXCH, 2, face, cases), F32),
            pltpu.VMEM((4, face), jnp.int32),
            pltpu.VMEM((5, owned, coarse), F32),
            pltpu.VMEM((nb + 2, owned, group), F32),
            pltpu.VMEM((nb, 3, owned, group), F32),
            pltpu.VMEM((nb * owned, group), BF16),
            pltpu.VMEM((nb * owned, group), BF16),
            pltpu.VMEM((ng, owned, 128), jnp.int32),
            pltpu.VMEM((4, owned, face), F32),
            pltpu.VMEM((4, owned, face), F32),
            pltpu.VMEM((4, 2 * owned, face), BF16),
            pltpu.VMEM((ITERS, 4, owned, cases), F32),
            pltpu.VMEM((ITERS, 4, owned, cases), F32),
            pltpu.VMEM((8, cases), F32),
            pltpu.VMEM((ITERS + 1, ng, owned + 8, cases), F32),
            pltpu.VMEM((ITERS + 1, nb, owned + 8, cases), F32),
            pltpu.VMEM((ITERS + 1, nb, owned + 8, cases), F32),
            pltpu.VMEM((1, cases), F32),
            pltpu.VMEM((1, cases), F32),
        ]
        + [dma((4,))]
        + [dma((EXCH, 4))] * 2
        + [dma((EXCH, 4))] * 2
        + [dma((EXCH, 2))]
        + [dma((1,))] * 2
        + [dma((4,))] * 2
        + [dma((1,))] * 4
        + [dma((ITERS + 1,))] * 4
        + [dma((4,))] * 2
        + [dma((ITERS, 4))] * 2
    )
    x, r = pl.pallas_call(
        functools.partial(kernel, sizes),
        out_shape=(shape, shape),
        in_specs=[vmem, hbm, hbm, vmem, vmem, smem, vmem],
        out_specs=(vmem, vmem),
        scratch_shapes=scratch,
        compiler_params=pltpu.CompilerParams(
            collective_id=0, has_side_effects=True, vmem_limit_bytes=56 * 1024 * 1024
        ),
        name="bddc_cg",
    )(
        loads[0, 0],
        schur[0, 0],
        local_inverse[0, 0],
        psi[0, 0].T,
        face_map[0, 0, 0],
        primal_list[0, 0, 0],
        coarse_inverse,
    )
    x, r = pl.pallas_call(
        deliver,
        out_shape=(shape, shape),
        in_specs=[vmem, vmem],
        out_specs=(vmem, vmem),
        name="deliver",
    )(x, r)
    return x[None, None], r[None, None]


def solution(mesh):
    sizes = tuple(mesh.shape[axis] for axis in ("blk", "mer", "ply"))
    in_specs = (
        P("blk", "mer", "ply", None),
        P("blk", "mer", "ply", None),
        P("blk", "mer", "ply", None),
        P("blk", "mer", "ply", None),
        P("blk", "mer", "ply", None, None),
        P("blk", "mer", "ply", None),
        P(("blk", "mer", "ply"), None),
    )
    out_specs = (P("blk", "mer", "ply", None), P("blk", "mer", "ply", None))
    return jax.shard_map(
        functools.partial(local, sizes), mesh=mesh, in_specs=in_specs, out_specs=out_specs, check_vma=False
    )
```

```python
import functools

import jax
import jax.numpy as jnp
from jax import lax
from jax.experimental import pallas as pl
from jax.experimental.pallas import tpu as pltpu
from jax.sharding import PartitionSpec as P

ITERS = 4
EXCH = 2 * ITERS + 1
F32 = jnp.float32
BF16 = jnp.bfloat16
HIGH = lax.Precision.HIGHEST
MESH = pl.DeviceIdType.MESH
NT = (((1,), (1,)), ((), ()))


def halves(value):
    hi = value.astype(BF16)
    return hi, (value - hi.astype(F32)).astype(BF16)


def thirds(value):
    hi = value.astype(BF16)
    rest = value - hi.astype(F32)
    mid = rest.astype(BF16)
    return hi, mid, (rest - mid.astype(F32)).astype(BF16)


def dot(left, right):
    return jnp.dot(left, right, preferred_element_type=F32)


def remote(src, dst, send, recv, device):
    return pltpu.make_async_remote_copy(
        src_ref=src, dst_ref=dst, send_sem=send, recv_sem=recv, device_id=device, device_id_type=MESH
    )


def kernel(
    sizes,
    loads_ref, schur_ref, linv_ref, psi_ref, map_ref, list_ref, coarse_ref,
    x_ref, r_ref,
    lf, sf, lhi, llo, shi, slo,
    face_tx, face_rx, own, ply_rx,
    pdir, simg, mdir, upre, raw, acc, tb, perm, psc, pst,
    fwd_tx, pmap, nbr, dpad, wblk, chi, clo, lists, psn_tx, psn_rx, psn, tsm_tx, tsm_rx,
    sums, co1, ytx, co2, rz_ref, pap_ref,
    load_sem, face_ss, face_rs, ply_ss, ply_rs, fwd_ss, map_ss, map_rs,
    nbr_ss, nbr_rs, win_ss, win_rs, list_ss, list_rs,
    co1_ss, co1_rs, co2_ss, co2_rs, psn_ss, psn_rs, tsm_ss, tsm_rs,
):
    nb, nm, npl = sizes
    ng = nm * npl
    half, cases = loads_ref.shape
    face = half // 4
    owned = coarse_ref.shape[0]
    b = lax.axis_index("blk")
    m = lax.axis_index("mer")
    p = lax.axis_index("ply")
    q = 1 - p
    mp = m * npl + p
    b_prev = lax.rem(b + nb - 1, nb)
    b_next = lax.rem(b + 1, nb)
    has_lo = m > 0
    has_hi = m < nm - 1
    weight = [
        0.5,
        0.5,
        jnp.where(has_lo, 0.5, 1.0).astype(F32),
        jnp.where(has_hi, 0.5, 1.0).astype(F32),
    ]
    partner = (b, m, q)
    neighbour = [(b_prev, m, p), (b_next, m, p), (b, m - 1, p), (b, m + 1, p)]
    exists = [None, None, has_lo, has_hi]
    run = nb // 2
    place = lax.rem(b, run)
    first = jnp.where(place < run // 2, 0, 1)
    second = 1 - first
    at_end = jnp.logical_or(place == 0, place == run - 1)
    toward_end = (jnp.where(first == 0, b_prev, b_next), m, p)
    from_end = (jnp.where(first == 0, b_next, b_prev), m, p)

    def device_at(f):
        if isinstance(f, int):
            return neighbour[f]
        return toward_end if f is first else from_end

    def opposite(f):
        return f ^ 1 if isinstance(f, int) else 1 - f

    def weight_of(f):
        return weight[f] if isinstance(f, int) else 0.5

    def guarded(f, fn):
        if not isinstance(f, int) or exists[f] is None:
            fn()
        else:
            pl.when(exists[f])(fn)

    mp_devices = [(b, i // npl, i % npl) for i in range(ng)]
    blk_devices = [(i, m, p) for i in range(nb)]

    def spread(me, devices, src_of, dst, send, recv):
        for i, device in enumerate(devices):
            pl.when(me != i)(lambda: remote(src_of(i), dst, send, recv, device).start())

    def fetch(index, source, side, target):
        column = pl.multiple_of(side * half, 128)
        return pltpu.make_async_copy(
            source.at[:, pl.ds(column, half)], target.at[index % 2], load_sem.at[index]
        )

    fetches = [
        fetch(0, linv_ref, p, lf),
        fetch(1, linv_ref, q, lf),
        fetch(2, schur_ref, p, sf),
        fetch(3, schur_ref, q, sf),
    ]
    for copy in fetches:
        copy.start()

    barrier = pltpu.get_barrier_semaphore()

    def greet(me, devices):
        for i, device in enumerate(devices):

            @pl.when(me != i)
            def _():
                pl.semaphore_signal(barrier, inc=1, device_id=device, device_id_type=MESH)

    greet(mp, mp_devices)
    greet(b, blk_devices)

    rows = lax.broadcasted_iota(jnp.int32, (face, face), 0)
    for f in range(4):
        perm[f] = jnp.where(rows == map_ref[f : f + 1, :], 1.0, 0.0).astype(BF16)

    for f in (2, 3):

        @pl.when(jnp.logical_not(exists[f]))
        def _():
            def clear(e, carry):
                face_rx[e, f] = jnp.zeros((face, cases), F32)
                return carry

            lax.fori_loop(0, EXCH, clear, 0)
            nbr[1 + f] = jnp.zeros(nbr.shape[1:], F32)
            for it in range(ITERS):
                tsm_rx[it, f] = jnp.zeros((owned, cases), F32)

    map_copy = remote(map_ref, pmap, map_ss.at[0], map_rs.at[0], partner)

    lane = lax.broadcasted_iota(jnp.int32, (owned, lists.shape[2]), 1)
    sub = lax.broadcasted_iota(jnp.int32, (owned, lists.shape[2]), 0)
    mine = jnp.zeros_like(lane)
    for k in range(owned):
        mine = jnp.where(sub == k, list_ref[k], mine)
    lists[mp] = mine

    def permute(f, value):
        hi, mid, lo = thirds(value)
        out = dot(perm[f], jnp.concatenate([hi, mid, lo], axis=1))
        return (out[:, 2 * cases :] + out[:, cases : 2 * cases]) + out[:, :cases]

    def face_copy(e, f):
        there = opposite(f)
        return remote(
            face_tx.at[e, f], face_rx.at[e, there], face_ss.at[e, f], face_rs.at[e, there], device_at(f)
        )

    def face_send(e, f):
        def go():
            face_tx[e, f] = permute(f, raw[f])
            face_copy(e, f).start()

        guarded(f, go)

    def faces_send(e):
        pl.when(at_end)(lambda: face_send(e, first))
        face_send(e, 2)
        face_send(e, 3)
        pl.when(jnp.logical_not(at_end))(lambda: face_send(e, first))
        face_send(e, second)

    def face_wait(e, f):
        guarded(
            f,
            lambda: remote(
                face_tx.at[e, f], face_rx.at[e, f], face_ss.at[e, f], face_rs.at[e, f], device_at(f)
            ).wait_recv(),
        )

    def faces_sent(e):
        for f in range(4):
            guarded(f, lambda f=f: face_copy(e, f).wait_send())

    def ply_copy(e, f):
        return remote(own.at[e, f], ply_rx.at[e, f], ply_ss.at[e, f], ply_rs.at[e, f], partner)

    def mer_forward(e):
        return remote(
            fwd_tx.at[e], ply_rx.at[e, 3], fwd_ss.at[e], ply_rs.at[e, 3], neighbour[2]
        )

    def when(condition, fn):
        pl.when(condition)(fn)

    def pass_mer(e):
        ply_copy(e, 2).wait_recv()

        @pl.when(has_lo)
        def _():
            fwd_tx[e] = permute(4, ply_rx[e, 2])
            mer_forward(e).start()

    def ply_sent(e):
        for f in (0, 1, 2):
            ply_copy(e, f).wait_send()
        when(jnp.logical_not(has_hi), lambda: ply_copy(e, 3).wait_send())
        when(has_lo, lambda: mer_forward(e).wait_send())

    def batch(buffer, index, count, send, recv):
        block = buffer.at[index, pl.ds(0, count - 1)]
        return remote(block, block, send, recv, partner)

    def group_first(it, terms):
        co1[it, mp, pl.ds(0, owned)] = terms
        co1[it, mp, pl.ds(owned, 8)] = sums[...]
        spread(mp, mp_devices, lambda _: co1.at[it, mp], co1.at[it, mp], co1_ss.at[it], co1_rs.at[it])

    def group_second(it, coarse):
        batch(co1, it, ng, co1_ss.at[it], co1_rs.at[it]).wait_recv()
        if coarse:
            high, low = halves(co1[it, :, pl.ds(0, owned)].reshape(ng * owned, cases))
            both = dot(chi[...], jnp.concatenate([high, low], axis=1))
            y = (both[:, :cases] + both[:, cases:]) + dot(clo[...], high)
            ytx[it, :, pl.ds(0, owned)] = y.reshape(nb, owned, cases)
        else:
            ytx[it, :, pl.ds(0, owned)] = jnp.zeros((nb, owned, cases), F32)
        inner = jnp.sum(co1[it, :, pl.ds(owned, 8)], axis=0)
        ytx[it, :, pl.ds(owned, 8)] = jnp.broadcast_to(inner[None], (nb, 8, cases))
        spread(b, blk_devices, lambda i: ytx.at[it, i], co2.at[it, b], co2_ss.at[it], co2_rs.at[it])
        co2[it, b] = ytx[it, b]

    def group_end(it):
        batch(co2, it, nb, co2_ss.at[it], co2_rs.at[it]).wait_recv()
        total = jnp.sum(co2[it], axis=0)
        return total[:owned], total[owned : owned + 1], total[owned + 1 : owned + 2], total[owned + 2 : owned + 3]

    def group_sent(it):
        batch(co1, it, ng, co1_ss.at[it], co1_rs.at[it]).wait_send()
        batch(co2, it, nb, co2_ss.at[it], co2_rs.at[it]).wait_send()

    def rows_sum(value):
        return jnp.sum(value.reshape(face // 8, 8, cases), axis=0)

    def put_sums(parts):
        flat = [jnp.sum(part, axis=0, keepdims=True) for part in parts]
        index = lax.broadcasted_iota(jnp.int32, (8, cases), 0)
        out = jnp.zeros((8, cases), F32)
        for i, part in enumerate(flat):
            out = jnp.where(index == i, part, out)
        sums[...] = out

    def store_split(side, f, value):
        hi, lo = halves(value)
        tb[side, f, :, pl.ds(0, cases)] = hi
        tb[side, f, :, pl.ds(cases, cases)] = lo

    def product(hi, lo, side, pair):
        part = pl.ds(2 * pair * face, 2 * face)
        vector = tb[side, pl.ds(2 * pair, 2)].reshape(2 * face, 2 * cases)
        both = dot(hi[side, :, part], vector)
        small = dot(lo[side, :, part], vector[:, :cases])
        return ((both[:, :cases] + both[:, cases:]) + small).reshape(4, face, cases)

    def terms_copy(it, f):
        there = opposite(f)
        return remote(
            tsm_tx.at[it, f], tsm_rx.at[it, there], tsm_ss.at[it, f], tsm_rs.at[it, there], device_at(f)
        )

    def three_parts(value):
        return value[:owned, :cases] + value[:owned, cases:] + value[owned:, :cases]

    def terms_send(it):
        for f in range(4):
            store_split(1, f, weight[f] * raw[f])
        for f in (0, 1, 2, 3):

            def go():
                tsm_tx[it, f] = three_parts(dot(psn[f], tb[1, f]))
                terms_copy(it, f).start()

            guarded(f, go)
        co1[it, mp, pl.ds(0, owned)] = three_parts(dot(pst[...], tb[1].reshape(half, 2 * cases)))

    def terms_end(it):
        total = co1[it, mp, pl.ds(0, owned)]
        for f in (2, 3, 0, 1):
            guarded(
                f,
                lambda: remote(
                    tsm_tx.at[it, f], tsm_rx.at[it, f], tsm_ss.at[it, f], tsm_rs.at[it, f], device_at(f)
                ).wait_recv(),
            )
            total += tsm_rx[it, f]
        return total

    def terms_sent(it):
        for f in range(4):
            guarded(f, lambda f=f: terms_copy(it, f).wait_send())

    psi_hi, psi_lo = halves(psi_ref[...])
    psi_hi, psi_lo = psi_hi.astype(F32), psi_lo.astype(F32)
    pst[...] = jnp.concatenate([psi_hi, psi_lo], axis=0).astype(BF16)
    three = jnp.concatenate([psi_hi, psi_hi, psi_lo], axis=0).astype(BF16)
    eye_r = lax.broadcasted_iota(jnp.int32, (3 * owned, 3 * owned), 0)
    eye_c = lax.broadcasted_iota(jnp.int32, (3 * owned, 3 * owned), 1)
    eye = jnp.where(eye_r == eye_c, 1.0, 0.0).astype(BF16)
    psc[...] = lax.dot_general(
        three, eye, (((0,), (0,)), ((), ())), preferred_element_type=F32
    ).astype(BF16)

    def split_matrix(source, hi, lo):
        def step(i, carry):
            part = pl.ds(i * 64, 64)
            for side in range(2):
                a, c = halves(source[side, part, :])
                hi[side, part, :] = a
                lo[side, part, :] = c
            return carry

        lax.fori_loop(0, half // 64, step, 0)

    group = ng * owned
    this = (b * nm + m) * npl + p
    bases = [
        this * owned,
        ((b_prev * nm + m) * npl + p) * owned,
        ((b_next * nm + m) * npl + p) * owned,
        jnp.where(has_lo, (this - npl) * owned, -owned),
        jnp.where(has_hi, (this + npl) * owned, -owned),
    ]
    wide = lax.broadcasted_iota(jnp.int32, (owned, 5 * owned), 1)
    tall = lax.broadcasted_iota(jnp.int32, (owned, 5 * owned), 0)
    names = jnp.zeros_like(wide)
    for t in range(5):
        names = jnp.where(lax.div(wide, owned) == t, bases[t] + wide - t * owned, names)
    slots = jnp.zeros_like(wide)
    for k in range(owned):
        slots = jnp.where(tall == k, list_ref[k], slots)
    selector = jnp.where(slots == names, 1.0, 0.0).astype(F32)
    pl.semaphore_wait(barrier, ng - 1 + nb - 1)

    slot_there = [2, 1, 4, 3]

    def nbr_copy(f):
        slot = slot_there[f]
        return remote(coarse_ref, nbr.at[slot], nbr_ss.at[f], nbr_rs.at[slot - 1], neighbour[f])

    for f in range(4):
        guarded(f, lambda f=f: nbr_copy(f).start())
    map_copy.start()
    nbr[0] = coarse_ref[...]
    spread(mp, mp_devices, lambda _: lists.at[mp], lists.at[mp], list_ss.at[0], list_rs.at[0])

    def psn_copy(f):
        there = opposite(f)
        return remote(psn_tx.at[f], psn_rx.at[there], psn_ss.at[f], psn_rs.at[there], device_at(f))

    for f in range(4):

        def go():
            hi, mid, lo = thirds(psi_ref[:, pl.ds(f * face, face)])
            stacked = jnp.concatenate(
                [hi.astype(F32), mid.astype(F32), lo.astype(F32)], axis=0
            ).astype(BF16)
            out = lax.dot_general(stacked, perm[f], NT, preferred_element_type=F32)
            psn_tx[f] = (out[2 * owned :] + out[owned : 2 * owned]) + out[:owned]
            psn_copy(f).start()

        guarded(f, go)

    for f in range(4):
        raw[f] = loads_ref[pl.ds(f * face, face), :]
    faces_send(0)

    for f in range(4):
        guarded(
            f,
            lambda f=f: remote(
                coarse_ref, nbr.at[1 + f], nbr_ss.at[f], nbr_rs.at[f], neighbour[f]
            ).wait_recv(),
        )
    hot = selector.astype(BF16)
    hi, mid, lo = thirds(nbr[...].reshape(5 * owned, nbr.shape[2]))
    named = (dot(hot, lo) + dot(hot, mid)) + dot(hot, hi)
    for j in range(nb + 2):
        block = (j - 1) % nb
        dpad[j] = named[:, block * group : (block + 1) * group]
    wblk[b] = dpad[pl.ds(b, 3)]
    spread(b, blk_devices, lambda peer: dpad.at[pl.ds(peer, 3)], wblk.at[b], win_ss.at[0], win_rs.at[0])

    for f in range(4):

        def go():
            remote(
                psn_tx.at[f], psn_rx.at[f], psn_ss.at[f], psn_rs.at[f], device_at(f)
            ).wait_recv()
            hi, lo = halves(psn_rx[f])
            psn[f] = jnp.concatenate([hi.astype(F32), lo.astype(F32)], axis=0).astype(BF16)

        guarded(f, go)
    terms_send(0)

    fetches[0].wait()
    fetches[1].wait()
    split_matrix(lf, lhi, llo)
    map_copy.wait_recv()
    perm[4] = jnp.where(rows == pmap[2:3, :], 1.0, 0.0).astype(BF16)
    for state in (x_ref, r_ref, pdir, simg, mdir, upre, pap_ref, sums):
        state[...] = jnp.zeros_like(state)
    rz_ref[...] = jnp.ones_like(rz_ref)

    def coarse_block():
        block = lists.at[pl.ds(0, ng - 1)]
        remote(block, block, list_ss.at[0], list_rs.at[0], partner).wait_recv()
        names = lists[:, :, pl.ds(0, group)].reshape(group, group)
        column = lax.broadcasted_iota(jnp.int32, (group, group), 1)
        block = wblk.at[pl.ds(0, nb - 1)]
        remote(block, block, win_ss.at[0], win_rs.at[0], partner).wait_recv()
        total = jnp.zeros((nb * owned, group), F32)
        for j, start in enumerate((b_prev, b, b_next)):
            hot = jnp.where(names == column + start * group, 1.0, 0.0).astype(BF16)
            window = wblk[:, j].reshape(nb * owned, group)
            hi, mid, lo = (
                lax.dot_general(piece, hot, NT, preferred_element_type=F32) for piece in thirds(window)
            )
            total += (lo + mid) + hi
        chi[...], clo[...] = halves(total)
        for f in range(4):
            guarded(f, lambda f=f: psn_copy(f).wait_send())
        for f in range(4):
            guarded(f, lambda f=f: nbr_copy(f).wait_send())
        block = lists.at[pl.ds(0, ng - 1)]
        remote(block, block, list_ss.at[0], list_rs.at[0], partner).wait_send()
        block = wblk.at[pl.ds(0, nb - 1)]
        remote(block, block, win_ss.at[0], win_rs.at[0], partner).wait_send()
        map_copy.wait_send()

    def assemble(e, f):
        face_wait(e, f)
        own[e, f] = raw[f] + face_rx[e, f]

    def exchange(e, hi, lo, weights, early, middle):
        def scaled(f, value):
            return value if weights is None else weight_of(f) * value

        def add(side, pair):
            acc[...] += product(hi, lo, side, pair)

        def pair_send(one, two):
            assemble(e, one)
            ply_copy(e, one).start()
            assemble(e, two)
            if isinstance(two, int):
                when(jnp.logical_not(has_hi), lambda: ply_copy(e, 3).start())
            else:
                ply_copy(e, two).start()

        def split(f):
            store_split(0, f, scaled(f, own[e, f]))

        pair_send(2, 3)
        early()
        split(2)
        split(3)
        acc[...] = product(hi, lo, 0, 1)

        @pl.when(jnp.logical_not(at_end))
        def _():
            pair_send(first, second)
            split(0)
            split(1)
            add(0, 0)

        @pl.when(at_end)
        def _():
            assemble(e, second)
            ply_copy(e, second).start()
            split(second)

        pass_mer(e)
        middle()

        @pl.when(at_end)
        def _():
            assemble(e, first)
            ply_copy(e, first).start()
            split(first)
            add(0, 0)

        ply_copy(e, 3).wait_recv()
        for pair in (1, 0):
            if pair == 0:
                ply_copy(e, second).wait_recv()
                ply_copy(e, first).wait_recv()
            for f in (2 * pair, 2 * pair + 1):
                store_split(1, f, scaled(f, ply_rx[e, f]))
            add(1, pair)

    def steps(it, rz, energy, cross):
        beta = jnp.where(it <= 1, 0.0, rz / rz_ref[...])
        pap = (energy + 2.0 * beta * cross) + beta * beta * pap_ref[...]
        alpha = jnp.where(it == 0, -1.0, rz / pap)

        @pl.when(it > 0)
        def _():
            rz_ref[...] = rz
            pap_ref[...] = pap

        return alpha, beta

    def advance(e, alpha, beta):
        for f in range(4):
            part = pl.ds(f * face, face)
            value = own[e, f] + beta * simg[f]
            simg[f] = value
            r_ref[part, :] -= alpha * value

        @pl.when(e > 0)
        def _():
            for f in range(4):
                value = own[e - 1, f] + beta * pdir[f]
                pdir[f] = value
                x_ref[pl.ds(f * face, face), :] += alpha * value

    def iteration(it, carry):
        e1 = 2 * it
        e2 = e1 + 1

        def early():
            group_first(it, terms_end(it))

        def middle():
            @pl.when(it == 0)
            def _():
                coarse_block()

            group_second(it, True)

            @pl.when(it == 0)
            def _():
                fetches[2].wait()
                fetches[3].wait()
                split_matrix(sf, shi, slo)

        exchange(e1, lhi, llo, weight, early, middle)
        picked, rz, energy, cross = group_end(it)
        pick_hi = picked.astype(BF16).astype(F32)
        stack = jnp.concatenate([pick_hi, picked - pick_hi, pick_hi], axis=0).astype(BF16)
        correction = dot(psc[...], stack).reshape(4, face, cases)
        alpha, beta = steps(it, rz, energy, cross)
        for f in range(4):
            change = (acc[f] + correction[f]) + beta * mdir[f]
            mdir[f] = change
            value = upre[f] - alpha * change
            upre[f] = value
            raw[f] = weight[f] * value
        faces_send(e2)
        advance(e1, alpha, beta)
        partial = jnp.zeros((8, cases), F32)
        for f in range(4):
            partial += rows_sum(raw[f] * r_ref[pl.ds(f * face, face), :])
        faces_sent(e1)
        ply_sent(e1)
        group_sent(it)
        terms_sent(it)

        exchange(e2, shi, slo, None, lambda: None, lambda: None)
        raw[...] = acc[...]
        pl.when(it + 1 < ITERS)(lambda: terms_send(it + 1))
        faces_send(e2 + 1)
        energy = jnp.zeros((8, cases), F32)
        cross = jnp.zeros((8, cases), F32)
        for f in range(4):
            energy += rows_sum(raw[f] * own[e2, f])
            cross += rows_sum(raw[f] * pdir[f])
        put_sums((partial, energy, cross))
        faces_sent(e2)
        ply_sent(e2)
        return carry

    lax.fori_loop(0, ITERS, iteration, 0)

    last = EXCH - 1
    group_first(ITERS, jnp.zeros((owned, cases), F32))
    assemble(last, 2)
    assemble(last, 3)
    group_second(ITERS, False)
    assemble(last, 0)
    assemble(last, 1)
    _, rz, energy, cross = group_end(ITERS)
    alpha, beta = steps(ITERS, rz, energy, cross)
    advance(last, alpha, beta)
    faces_sent(last)
    group_sent(ITERS)


def deliver(x_ref, r_ref, x_out, r_out):
    x_out[...] = x_ref[...]
    r_out[...] = r_ref[...]


def local(sizes, loads, schur, local_inverse, psi, face_map, primal_list, coarse_inverse):
    nb, nm, npl = sizes
    ng = nm * npl
    half, cases = loads.shape[2:]
    face = half // 4
    owned, coarse = coarse_inverse.shape
    group = ng * owned
    shape = jax.ShapeDtypeStruct((half, cases), F32)
    vmem = pl.BlockSpec(memory_space=pltpu.VMEM)
    smem = pl.BlockSpec(memory_space=pltpu.SMEM)
    hbm = pl.BlockSpec(memory_space=pl.ANY)
    faces = (4, face, cases)
    dma = pltpu.SemaphoreType.DMA
    scratch = (
        [pltpu.VMEM((2, half, half), F32)] * 2
        + [pltpu.VMEM((2, half, half), BF16)] * 4
        + [pltpu.VMEM((EXCH,) + faces, F32)] * 4
        + [pltpu.VMEM(faces, F32)] * 5
        + [
            pltpu.VMEM(faces, F32),
            pltpu.VMEM((2, 4, face, 2 * cases), BF16),
            pltpu.VMEM((5, face, face), BF16),
            pltpu.VMEM((half, 3 * owned), BF16),
            pltpu.VMEM((2 * owned, half), BF16),
            pltpu.VMEM((EXCH, face, cases), F32),
            pltpu.VMEM((4, face), jnp.int32),
            pltpu.VMEM((5, owned, coarse), F32),
            pltpu.VMEM((nb + 2, owned, group), F32),
            pltpu.VMEM((nb, 3, owned, group), F32),
            pltpu.VMEM((nb * owned, group), BF16),
            pltpu.VMEM((nb * owned, group), BF16),
            pltpu.VMEM((ng, owned, 128), jnp.int32),
            pltpu.VMEM((4, owned, face), F32),
            pltpu.VMEM((4, owned, face), F32),
            pltpu.VMEM((4, 2 * owned, face), BF16),
            pltpu.VMEM((ITERS, 4, owned, cases), F32),
            pltpu.VMEM((ITERS, 4, owned, cases), F32),
            pltpu.VMEM((8, cases), F32),
            pltpu.VMEM((ITERS + 1, ng, owned + 8, cases), F32),
            pltpu.VMEM((ITERS + 1, nb, owned + 8, cases), F32),
            pltpu.VMEM((ITERS + 1, nb, owned + 8, cases), F32),
            pltpu.VMEM((1, cases), F32),
            pltpu.VMEM((1, cases), F32),
        ]
        + [dma((4,))]
        + [dma((EXCH, 4))] * 2
        + [dma((EXCH, 4))] * 2
        + [dma((EXCH,))]
        + [dma((1,))] * 2
        + [dma((4,))] * 2
        + [dma((1,))] * 4
        + [dma((ITERS + 1,))] * 4
        + [dma((4,))] * 2
        + [dma((ITERS, 4))] * 2
    )
    x, r = pl.pallas_call(
        functools.partial(kernel, sizes),
        out_shape=(shape, shape),
        in_specs=[vmem, hbm, hbm, vmem, vmem, smem, vmem],
        out_specs=(vmem, vmem),
        scratch_shapes=scratch,
        compiler_params=pltpu.CompilerParams(
            collective_id=0, has_side_effects=True, vmem_limit_bytes=56 * 1024 * 1024
        ),
        name="bddc_cg",
    )(
        loads[0, 0],
        schur[0, 0],
        local_inverse[0, 0],
        psi[0, 0].T,
        face_map[0, 0, 0],
        primal_list[0, 0, 0],
        coarse_inverse,
    )
    x, r = pl.pallas_call(
        deliver,
        out_shape=(shape, shape),
        in_specs=[vmem, vmem],
        out_specs=(vmem, vmem),
        name="deliver",
    )(x, r)
    return x[None, None], r[None, None]


def solution(mesh):
    sizes = tuple(mesh.shape[axis] for axis in ("blk", "mer", "ply"))
    in_specs = (
        P("blk", "mer", "ply", None),
        P("blk", "mer", "ply", None),
        P("blk", "mer", "ply", None),
        P("blk", "mer", "ply", None),
        P("blk", "mer", "ply", None, None),
        P("blk", "mer", "ply", None),
        P(("blk", "mer", "ply"), None),
    )
    out_specs = (P("blk", "mer", "ply", None), P("blk", "mer", "ply", None))
    return jax.shard_map(
        functools.partial(local, sizes), mesh=mesh, in_specs=in_specs, out_specs=out_specs, check_vma=False
    )
```

```python
import functools

import jax
import jax.numpy as jnp
from jax import lax
from jax.experimental import pallas as pl
from jax.experimental.pallas import tpu as pltpu
from jax.sharding import PartitionSpec as P

ITERS = 4
EXCH = 2 * ITERS + 1
F32 = jnp.float32
BF16 = jnp.bfloat16
HIGH = lax.Precision.HIGHEST
MESH = pl.DeviceIdType.MESH
NT = (((1,), (1,)), ((), ()))


def halves(value):
    hi = value.astype(BF16)
    return hi, (value - hi.astype(F32)).astype(BF16)


def thirds(value):
    hi = value.astype(BF16)
    rest = value - hi.astype(F32)
    mid = rest.astype(BF16)
    return hi, mid, (rest - mid.astype(F32)).astype(BF16)


def dot(left, right):
    return jnp.dot(left, right, preferred_element_type=F32)


def remote(src, dst, send, recv, device):
    return pltpu.make_async_remote_copy(
        src_ref=src, dst_ref=dst, send_sem=send, recv_sem=recv, device_id=device, device_id_type=MESH
    )


def kernel(
    sizes,
    loads_ref, schur_ref, linv_ref, psi_ref, map_ref, list_ref, coarse_ref,
    x_ref, r_ref,
    lf, sf, lhi, llo, shi, slo,
    face_tx, face_rx, own, ply_rx,
    pdir, simg, mdir, upre, raw, acc, tb, perm, psc, pst,
    fwd_tx, far_tx, far_rx, pmap, nbr, dpad, wblk, chi, clo, lists, psn_tx, psn_rx, psn, tsm_tx, tsm_rx,
    sums, co1, ytx, co2, rz_ref, pap_ref,
    load_sem, face_ss, face_rs, ply_ss, ply_rs, fwd_ss, map_ss, map_rs,
    nbr_ss, nbr_rs, win_ss, win_rs, list_ss, list_rs,
    co1_ss, co1_rs, co2_ss, co2_rs, psn_ss, psn_rs, tsm_ss, tsm_rs, far_ss, far_rs,
):
    nb, nm, npl = sizes
    ng = nm * npl
    half, cases = loads_ref.shape
    face = half // 4
    owned = coarse_ref.shape[0]
    b = lax.axis_index("blk")
    m = lax.axis_index("mer")
    p = lax.axis_index("ply")
    q = 1 - p
    mp = m * npl + p
    b_prev = lax.rem(b + nb - 1, nb)
    b_next = lax.rem(b + 1, nb)
    has_lo = m > 0
    has_hi = m < nm - 1
    weight = [
        0.5,
        0.5,
        jnp.where(has_lo, 0.5, 1.0).astype(F32),
        jnp.where(has_hi, 0.5, 1.0).astype(F32),
    ]
    partner = (b, m, q)
    neighbour = [(b_prev, m, p), (b_next, m, p), (b, m - 1, p), (b, m + 1, p)]
    exists = [None, None, has_lo, has_hi]
    run = nb // 2
    place = lax.rem(b, run)
    first = jnp.where(place < run // 2, 0, 1)
    second = 1 - first
    at_end = jnp.logical_or(place == 0, place == run - 1)
    toward_end = (jnp.where(first == 0, b_prev, b_next), m, p)
    from_end = (jnp.where(first == 0, b_next, b_prev), m, p)
    across_end = (jnp.where(first == 0, b_prev, b_next), m, q)

    def device_at(f):
        if isinstance(f, int):
            return neighbour[f]
        return toward_end if f is first else from_end

    def opposite(f):
        return f ^ 1 if isinstance(f, int) else 1 - f

    def weight_of(f):
        return weight[f] if isinstance(f, int) else 0.5

    def guarded(f, fn):
        if not isinstance(f, int) or exists[f] is None:
            fn()
        else:
            pl.when(exists[f])(fn)

    mp_devices = [(b, i // npl, i % npl) for i in range(ng)]
    blk_devices = [(i, m, p) for i in range(nb)]

    def spread(me, devices, src_of, dst, send, recv):
        for i, device in enumerate(devices):
            pl.when(me != i)(lambda: remote(src_of(i), dst, send, recv, device).start())

    def fetch(index, source, side, target):
        column = pl.multiple_of(side * half, 128)
        return pltpu.make_async_copy(
            source.at[:, pl.ds(column, half)], target.at[index % 2], load_sem.at[index]
        )

    fetches = [
        fetch(0, linv_ref, p, lf),
        fetch(1, linv_ref, q, lf),
        fetch(2, schur_ref, p, sf),
        fetch(3, schur_ref, q, sf),
    ]
    for copy in fetches:
        copy.start()

    barrier = pltpu.get_barrier_semaphore()

    def greet(me, devices):
        for i, device in enumerate(devices):

            @pl.when(me != i)
            def _():
                pl.semaphore_signal(barrier, inc=1, device_id=device, device_id_type=MESH)

    greet(mp, mp_devices)
    greet(b, blk_devices)

    @pl.when(at_end)
    def _():
        pl.semaphore_signal(barrier, inc=1, device_id=across_end, device_id_type=MESH)

    rows = lax.broadcasted_iota(jnp.int32, (face, face), 0)
    for f in range(4):
        perm[f] = jnp.where(rows == map_ref[f : f + 1, :], 1.0, 0.0).astype(BF16)

    for f in (2, 3):

        @pl.when(jnp.logical_not(exists[f]))
        def _():
            def clear(e, carry):
                face_rx[e, f] = jnp.zeros((face, cases), F32)
                return carry

            lax.fori_loop(0, EXCH, clear, 0)
            nbr[1 + f] = jnp.zeros(nbr.shape[1:], F32)
            for it in range(ITERS):
                tsm_rx[it, f] = jnp.zeros((owned, cases), F32)

    map_copy = remote(map_ref, pmap, map_ss.at[0], map_rs.at[0], partner)

    lane = lax.broadcasted_iota(jnp.int32, (owned, lists.shape[2]), 1)
    sub = lax.broadcasted_iota(jnp.int32, (owned, lists.shape[2]), 0)
    mine = jnp.zeros_like(lane)
    for k in range(owned):
        mine = jnp.where(sub == k, list_ref[k], mine)
    lists[mp] = mine

    def permute(f, value):
        hi, mid, lo = thirds(value)
        out = dot(perm[f], jnp.concatenate([hi, mid, lo], axis=1))
        return (out[:, 2 * cases :] + out[:, cases : 2 * cases]) + out[:, :cases]

    def face_copy(e, f):
        there = opposite(f)
        return remote(
            face_tx.at[e, f], face_rx.at[e, there], face_ss.at[e, f], face_rs.at[e, there], device_at(f)
        )

    def face_send(e, f):
        def go():
            face_tx[e, f] = permute(f, raw[f])
            face_copy(e, f).start()

        guarded(f, go)

    def across_copy(e):
        return remote(face_tx.at[e, first], far_rx.at[e], far_ss.at[e], far_rs.at[e], across_end)

    def far_copy(e):
        return remote(far_tx.at[e], ply_rx.at[e, first], ply_ss.at[e, first], ply_rs.at[e, first], partner)

    def faces_send(e):
        @pl.when(at_end)
        def _():
            face_send(e, first)

            @pl.when(e < EXCH - 1)
            def _():
                across_copy(e).start()
                far_tx[e] = raw[first]
                far_copy(e).start()

        face_send(e, 2)
        face_send(e, 3)
        pl.when(jnp.logical_not(at_end))(lambda: face_send(e, first))
        face_send(e, second)

    def face_wait(e, f):
        guarded(
            f,
            lambda: remote(
                face_tx.at[e, f], face_rx.at[e, f], face_ss.at[e, f], face_rs.at[e, f], device_at(f)
            ).wait_recv(),
        )

    def faces_sent(e):
        for f in range(4):
            guarded(f, lambda f=f: face_copy(e, f).wait_send())

    def ply_copy(e, f):
        return remote(own.at[e, f], ply_rx.at[e, f], ply_ss.at[e, f], ply_rs.at[e, f], partner)

    def mer_forward(e):
        return remote(
            fwd_tx.at[e], ply_rx.at[e, 3], fwd_ss.at[e], ply_rs.at[e, 3], neighbour[2]
        )

    def when(condition, fn):
        pl.when(condition)(fn)

    def pass_mer(e):
        ply_copy(e, 2).wait_recv()

        @pl.when(has_lo)
        def _():
            fwd_tx[e] = permute(4, ply_rx[e, 2])
            mer_forward(e).start()

    def ply_sent(e):
        ply_copy(e, second).wait_send()
        ply_copy(e, 2).wait_send()
        when(jnp.logical_not(at_end), lambda: ply_copy(e, first).wait_send())

        @pl.when(at_end)
        def _():
            far_copy(e).wait_send()
            across_copy(e).wait_send()

        when(jnp.logical_not(has_hi), lambda: ply_copy(e, 3).wait_send())
        when(has_lo, lambda: mer_forward(e).wait_send())

    def batch(buffer, index, count, send, recv):
        block = buffer.at[index, pl.ds(0, count - 1)]
        return remote(block, block, send, recv, partner)

    def group_first(it, terms):
        co1[it, mp, pl.ds(0, owned)] = terms
        co1[it, mp, pl.ds(owned, 8)] = sums[...]
        spread(mp, mp_devices, lambda _: co1.at[it, mp], co1.at[it, mp], co1_ss.at[it], co1_rs.at[it])

    def group_second(it, coarse):
        batch(co1, it, ng, co1_ss.at[it], co1_rs.at[it]).wait_recv()
        if coarse:
            high, low = halves(co1[it, :, pl.ds(0, owned)].reshape(ng * owned, cases))
            both = dot(chi[...], jnp.concatenate([high, low], axis=1))
            y = (both[:, :cases] + both[:, cases:]) + dot(clo[...], high)
            ytx[it, :, pl.ds(0, owned)] = y.reshape(nb, owned, cases)
        else:
            ytx[it, :, pl.ds(0, owned)] = jnp.zeros((nb, owned, cases), F32)
        inner = jnp.sum(co1[it, :, pl.ds(owned, 8)], axis=0)
        ytx[it, :, pl.ds(owned, 8)] = jnp.broadcast_to(inner[None], (nb, 8, cases))
        spread(b, blk_devices, lambda i: ytx.at[it, i], co2.at[it, b], co2_ss.at[it], co2_rs.at[it])
        co2[it, b] = ytx[it, b]

    def group_end(it):
        batch(co2, it, nb, co2_ss.at[it], co2_rs.at[it]).wait_recv()
        total = jnp.sum(co2[it], axis=0)
        return total[:owned], total[owned : owned + 1], total[owned + 1 : owned + 2], total[owned + 2 : owned + 3]

    def group_sent(it):
        batch(co1, it, ng, co1_ss.at[it], co1_rs.at[it]).wait_send()
        batch(co2, it, nb, co2_ss.at[it], co2_rs.at[it]).wait_send()

    def rows_sum(value):
        return jnp.sum(value.reshape(face // 8, 8, cases), axis=0)

    def put_sums(parts):
        flat = [jnp.sum(part, axis=0, keepdims=True) for part in parts]
        index = lax.broadcasted_iota(jnp.int32, (8, cases), 0)
        out = jnp.zeros((8, cases), F32)
        for i, part in enumerate(flat):
            out = jnp.where(index == i, part, out)
        sums[...] = out

    def store_split(side, f, value):
        hi, lo = halves(value)
        tb[side, f, :, pl.ds(0, cases)] = hi
        tb[side, f, :, pl.ds(cases, cases)] = lo

    def product(hi, lo, side, pair):
        part = pl.ds(2 * pair * face, 2 * face)
        vector = tb[side, pl.ds(2 * pair, 2)].reshape(2 * face, 2 * cases)
        both = dot(hi[side, :, part], vector)
        small = dot(lo[side, :, part], vector[:, :cases])
        return ((both[:, :cases] + both[:, cases:]) + small).reshape(4, face, cases)

    def terms_copy(it, f):
        there = opposite(f)
        return remote(
            tsm_tx.at[it, f], tsm_rx.at[it, there], tsm_ss.at[it, f], tsm_rs.at[it, there], device_at(f)
        )

    def three_parts(value):
        return value[:owned, :cases] + value[:owned, cases:] + value[owned:, :cases]

    def terms_send(it):
        for f in range(4):
            store_split(1, f, weight[f] * raw[f])
        for f in (0, 1, 2, 3):

            def go():
                tsm_tx[it, f] = three_parts(dot(psn[f], tb[1, f]))
                terms_copy(it, f).start()

            guarded(f, go)
        co1[it, mp, pl.ds(0, owned)] = three_parts(dot(pst[...], tb[1].reshape(half, 2 * cases)))

    def terms_end(it):
        total = co1[it, mp, pl.ds(0, owned)]
        for f in (2, 3, 0, 1):
            guarded(
                f,
                lambda: remote(
                    tsm_tx.at[it, f], tsm_rx.at[it, f], tsm_ss.at[it, f], tsm_rs.at[it, f], device_at(f)
                ).wait_recv(),
            )
            total += tsm_rx[it, f]
        return total

    def terms_sent(it):
        for f in range(4):
            guarded(f, lambda f=f: terms_copy(it, f).wait_send())

    psi_hi, psi_lo = halves(psi_ref[...])
    psi_hi, psi_lo = psi_hi.astype(F32), psi_lo.astype(F32)
    pst[...] = jnp.concatenate([psi_hi, psi_lo], axis=0).astype(BF16)
    three = jnp.concatenate([psi_hi, psi_hi, psi_lo], axis=0).astype(BF16)
    eye_r = lax.broadcasted_iota(jnp.int32, (3 * owned, 3 * owned), 0)
    eye_c = lax.broadcasted_iota(jnp.int32, (3 * owned, 3 * owned), 1)
    eye = jnp.where(eye_r == eye_c, 1.0, 0.0).astype(BF16)
    psc[...] = lax.dot_general(
        three, eye, (((0,), (0,)), ((), ())), preferred_element_type=F32
    ).astype(BF16)

    def split_matrix(source, hi, lo):
        def step(i, carry):
            part = pl.ds(i * 64, 64)
            for side in range(2):
                a, c = halves(source[side, part, :])
                hi[side, part, :] = a
                lo[side, part, :] = c
            return carry

        lax.fori_loop(0, half // 64, step, 0)

    group = ng * owned
    this = (b * nm + m) * npl + p
    bases = [
        this * owned,
        ((b_prev * nm + m) * npl + p) * owned,
        ((b_next * nm + m) * npl + p) * owned,
        jnp.where(has_lo, (this - npl) * owned, -owned),
        jnp.where(has_hi, (this + npl) * owned, -owned),
    ]
    wide = lax.broadcasted_iota(jnp.int32, (owned, 5 * owned), 1)
    tall = lax.broadcasted_iota(jnp.int32, (owned, 5 * owned), 0)
    names = jnp.zeros_like(wide)
    for t in range(5):
        names = jnp.where(lax.div(wide, owned) == t, bases[t] + wide - t * owned, names)
    slots = jnp.zeros_like(wide)
    for k in range(owned):
        slots = jnp.where(tall == k, list_ref[k], slots)
    selector = jnp.where(slots == names, 1.0, 0.0).astype(F32)
    pl.semaphore_wait(barrier, ng - 1 + nb - 1 + jnp.where(at_end, 1, 0))

    slot_there = [2, 1, 4, 3]

    def nbr_copy(f):
        slot = slot_there[f]
        return remote(coarse_ref, nbr.at[slot], nbr_ss.at[f], nbr_rs.at[slot - 1], neighbour[f])

    for f in range(4):
        guarded(f, lambda f=f: nbr_copy(f).start())
    map_copy.start()
    nbr[0] = coarse_ref[...]
    spread(mp, mp_devices, lambda _: lists.at[mp], lists.at[mp], list_ss.at[0], list_rs.at[0])

    def psn_copy(f):
        there = opposite(f)
        return remote(psn_tx.at[f], psn_rx.at[there], psn_ss.at[f], psn_rs.at[there], device_at(f))

    for f in range(4):

        def go():
            hi, mid, lo = thirds(psi_ref[:, pl.ds(f * face, face)])
            stacked = jnp.concatenate(
                [hi.astype(F32), mid.astype(F32), lo.astype(F32)], axis=0
            ).astype(BF16)
            out = lax.dot_general(stacked, perm[f], NT, preferred_element_type=F32)
            psn_tx[f] = (out[2 * owned :] + out[owned : 2 * owned]) + out[:owned]
            psn_copy(f).start()

        guarded(f, go)

    for f in range(4):
        raw[f] = loads_ref[pl.ds(f * face, face), :]
    faces_send(0)

    for f in range(4):
        guarded(
            f,
            lambda f=f: remote(
                coarse_ref, nbr.at[1 + f], nbr_ss.at[f], nbr_rs.at[f], neighbour[f]
            ).wait_recv(),
        )
    hot = selector.astype(BF16)
    hi, mid, lo = thirds(nbr[...].reshape(5 * owned, nbr.shape[2]))
    named = (dot(hot, lo) + dot(hot, mid)) + dot(hot, hi)
    for j in range(nb + 2):
        block = (j - 1) % nb
        dpad[j] = named[:, block * group : (block + 1) * group]
    wblk[b] = dpad[pl.ds(b, 3)]
    spread(b, blk_devices, lambda peer: dpad.at[pl.ds(peer, 3)], wblk.at[b], win_ss.at[0], win_rs.at[0])

    for f in range(4):

        def go():
            remote(
                psn_tx.at[f], psn_rx.at[f], psn_ss.at[f], psn_rs.at[f], device_at(f)
            ).wait_recv()
            hi, lo = halves(psn_rx[f])
            psn[f] = jnp.concatenate([hi.astype(F32), lo.astype(F32)], axis=0).astype(BF16)

        guarded(f, go)
    terms_send(0)

    fetches[0].wait()
    fetches[1].wait()
    split_matrix(lf, lhi, llo)
    map_copy.wait_recv()
    perm[4] = jnp.where(rows == pmap[2:3, :], 1.0, 0.0).astype(BF16)
    for state in (x_ref, r_ref, pdir, simg, mdir, upre, pap_ref, sums):
        state[...] = jnp.zeros_like(state)
    rz_ref[...] = jnp.ones_like(rz_ref)

    def coarse_block():
        block = lists.at[pl.ds(0, ng - 1)]
        remote(block, block, list_ss.at[0], list_rs.at[0], partner).wait_recv()
        names = lists[:, :, pl.ds(0, group)].reshape(group, group)
        column = lax.broadcasted_iota(jnp.int32, (group, group), 1)
        block = wblk.at[pl.ds(0, nb - 1)]
        remote(block, block, win_ss.at[0], win_rs.at[0], partner).wait_recv()
        total = jnp.zeros((nb * owned, group), F32)
        for j, start in enumerate((b_prev, b, b_next)):
            hot = jnp.where(names == column + start * group, 1.0, 0.0).astype(BF16)
            window = wblk[:, j].reshape(nb * owned, group)
            hi, mid, lo = (
                lax.dot_general(piece, hot, NT, preferred_element_type=F32) for piece in thirds(window)
            )
            total += (lo + mid) + hi
        chi[...], clo[...] = halves(total)
        for f in range(4):
            guarded(f, lambda f=f: psn_copy(f).wait_send())
        for f in range(4):
            guarded(f, lambda f=f: nbr_copy(f).wait_send())
        block = lists.at[pl.ds(0, ng - 1)]
        remote(block, block, list_ss.at[0], list_rs.at[0], partner).wait_send()
        block = wblk.at[pl.ds(0, nb - 1)]
        remote(block, block, win_ss.at[0], win_rs.at[0], partner).wait_send()
        map_copy.wait_send()

    def assemble(e, f):
        face_wait(e, f)
        own[e, f] = raw[f] + face_rx[e, f]

    def exchange(e, hi, lo, weights, early, middle):
        def scaled(f, value):
            return value if weights is None else weight_of(f) * value

        def add(side, pair):
            acc[...] += product(hi, lo, side, pair)

        def pair_send(one, two):
            assemble(e, one)
            ply_copy(e, one).start()
            assemble(e, two)
            if isinstance(two, int):
                when(jnp.logical_not(has_hi), lambda: ply_copy(e, 3).start())
            else:
                ply_copy(e, two).start()

        def split(f):
            store_split(0, f, scaled(f, own[e, f]))

        pair_send(2, 3)
        early()
        split(2)
        split(3)
        acc[...] = product(hi, lo, 0, 1)

        @pl.when(jnp.logical_not(at_end))
        def _():
            pair_send(first, second)
            split(0)
            split(1)
            add(0, 0)

        @pl.when(at_end)
        def _():
            assemble(e, second)
            ply_copy(e, second).start()
            split(second)

        pass_mer(e)
        middle()

        @pl.when(at_end)
        def _():
            assemble(e, first)
            split(first)
            add(0, 0)

        ply_copy(e, 3).wait_recv()
        for pair in (1, 0):
            if pair == 0:
                ply_copy(e, second).wait_recv()
                ply_copy(e, first).wait_recv()

                @pl.when(at_end)
                def _():
                    across_copy(e).wait_recv()
                    ply_rx[e, first] += far_rx[e]

            for f in (2 * pair, 2 * pair + 1):
                store_split(1, f, scaled(f, ply_rx[e, f]))
            add(1, pair)

    def steps(it, rz, energy, cross):
        beta = jnp.where(it <= 1, 0.0, rz / rz_ref[...])
        pap = (energy + 2.0 * beta * cross) + beta * beta * pap_ref[...]
        alpha = jnp.where(it == 0, -1.0, rz / pap)

        @pl.when(it > 0)
        def _():
            rz_ref[...] = rz
            pap_ref[...] = pap

        return alpha, beta

    def advance(e, alpha, beta):
        for f in range(4):
            part = pl.ds(f * face, face)
            value = own[e, f] + beta * simg[f]
            simg[f] = value
            r_ref[part, :] -= alpha * value

        @pl.when(e > 0)
        def _():
            for f in range(4):
                value = own[e - 1, f] + beta * pdir[f]
                pdir[f] = value
                x_ref[pl.ds(f * face, face), :] += alpha * value

    def iteration(it, carry):
        e1 = 2 * it
        e2 = e1 + 1

        def early():
            group_first(it, terms_end(it))

        def middle():
            @pl.when(it == 0)
            def _():
                coarse_block()

            group_second(it, True)

            @pl.when(it == 0)
            def _():
                fetches[2].wait()
                fetches[3].wait()
                split_matrix(sf, shi, slo)

        exchange(e1, lhi, llo, weight, early, middle)
        picked, rz, energy, cross = group_end(it)
        pick_hi = picked.astype(BF16).astype(F32)
        stack = jnp.concatenate([pick_hi, picked - pick_hi, pick_hi], axis=0).astype(BF16)
        correction = dot(psc[...], stack).reshape(4, face, cases)
        alpha, beta = steps(it, rz, energy, cross)
        for f in range(4):
            change = (acc[f] + correction[f]) + beta * mdir[f]
            mdir[f] = change
            value = upre[f] - alpha * change
            upre[f] = value
            raw[f] = weight[f] * value
        faces_send(e2)
        advance(e1, alpha, beta)
        partial = jnp.zeros((8, cases), F32)
        for f in range(4):
            partial += rows_sum(raw[f] * r_ref[pl.ds(f * face, face), :])
        faces_sent(e1)
        ply_sent(e1)
        group_sent(it)
        terms_sent(it)

        exchange(e2, shi, slo, None, lambda: None, lambda: None)
        raw[...] = acc[...]
        pl.when(it + 1 < ITERS)(lambda: terms_send(it + 1))
        faces_send(e2 + 1)
        energy = jnp.zeros((8, cases), F32)
        cross = jnp.zeros((8, cases), F32)
        for f in range(4):
            energy += rows_sum(raw[f] * own[e2, f])
            cross += rows_sum(raw[f] * pdir[f])
        put_sums((partial, energy, cross))
        faces_sent(e2)
        ply_sent(e2)
        return carry

    lax.fori_loop(0, ITERS, iteration, 0)

    last = EXCH - 1
    group_first(ITERS, jnp.zeros((owned, cases), F32))
    assemble(last, 2)
    assemble(last, 3)
    group_second(ITERS, False)
    assemble(last, 0)
    assemble(last, 1)
    _, rz, energy, cross = group_end(ITERS)
    alpha, beta = steps(ITERS, rz, energy, cross)
    advance(last, alpha, beta)
    faces_sent(last)
    group_sent(ITERS)


def deliver(x_ref, r_ref, x_out, r_out):
    x_out[...] = x_ref[...]
    r_out[...] = r_ref[...]


def local(sizes, loads, schur, local_inverse, psi, face_map, primal_list, coarse_inverse):
    nb, nm, npl = sizes
    ng = nm * npl
    half, cases = loads.shape[2:]
    face = half // 4
    owned, coarse = coarse_inverse.shape
    group = ng * owned
    shape = jax.ShapeDtypeStruct((half, cases), F32)
    vmem = pl.BlockSpec(memory_space=pltpu.VMEM)
    smem = pl.BlockSpec(memory_space=pltpu.SMEM)
    hbm = pl.BlockSpec(memory_space=pl.ANY)
    faces = (4, face, cases)
    dma = pltpu.SemaphoreType.DMA
    scratch = (
        [pltpu.VMEM((2, half, half), F32)] * 2
        + [pltpu.VMEM((2, half, half), BF16)] * 4
        + [pltpu.VMEM((EXCH,) + faces, F32)] * 4
        + [pltpu.VMEM(faces, F32)] * 5
        + [
            pltpu.VMEM(faces, F32),
            pltpu.VMEM((2, 4, face, 2 * cases), BF16),
            pltpu.VMEM((5, face, face), BF16),
            pltpu.VMEM((half, 3 * owned), BF16),
            pltpu.VMEM((2 * owned, half), BF16),
            pltpu.VMEM((EXCH, face, cases), F32),
            pltpu.VMEM((EXCH, face, cases), F32),
            pltpu.VMEM((EXCH, face, cases), F32),
            pltpu.VMEM((4, face), jnp.int32),
            pltpu.VMEM((5, owned, coarse), F32),
            pltpu.VMEM((nb + 2, owned, group), F32),
            pltpu.VMEM((nb, 3, owned, group), F32),
            pltpu.VMEM((nb * owned, group), BF16),
            pltpu.VMEM((nb * owned, group), BF16),
            pltpu.VMEM((ng, owned, 128), jnp.int32),
            pltpu.VMEM((4, owned, face), F32),
            pltpu.VMEM((4, owned, face), F32),
            pltpu.VMEM((4, 2 * owned, face), BF16),
            pltpu.VMEM((ITERS, 4, owned, cases), F32),
            pltpu.VMEM((ITERS, 4, owned, cases), F32),
            pltpu.VMEM((8, cases), F32),
            pltpu.VMEM((ITERS + 1, ng, owned + 8, cases), F32),
            pltpu.VMEM((ITERS + 1, nb, owned + 8, cases), F32),
            pltpu.VMEM((ITERS + 1, nb, owned + 8, cases), F32),
            pltpu.VMEM((1, cases), F32),
            pltpu.VMEM((1, cases), F32),
        ]
        + [dma((4,))]
        + [dma((EXCH, 4))] * 2
        + [dma((EXCH, 4))] * 2
        + [dma((EXCH,))]
        + [dma((1,))] * 2
        + [dma((4,))] * 2
        + [dma((1,))] * 4
        + [dma((ITERS + 1,))] * 4
        + [dma((4,))] * 2
        + [dma((ITERS, 4))] * 2
        + [dma((EXCH,))] * 2
    )
    x, r = pl.pallas_call(
        functools.partial(kernel, sizes),
        out_shape=(shape, shape),
        in_specs=[vmem, hbm, hbm, vmem, vmem, smem, vmem],
        out_specs=(vmem, vmem),
        scratch_shapes=scratch,
        compiler_params=pltpu.CompilerParams(
            collective_id=0, has_side_effects=True, vmem_limit_bytes=56 * 1024 * 1024
        ),
        name="bddc_cg",
    )(
        loads[0, 0],
        schur[0, 0],
        local_inverse[0, 0],
        psi[0, 0].T,
        face_map[0, 0, 0],
        primal_list[0, 0, 0],
        coarse_inverse,
    )
    x, r = pl.pallas_call(
        deliver,
        out_shape=(shape, shape),
        in_specs=[vmem, vmem],
        out_specs=(vmem, vmem),
        name="deliver",
    )(x, r)
    return x[None, None], r[None, None]


def solution(mesh):
    sizes = tuple(mesh.shape[axis] for axis in ("blk", "mer", "ply"))
    in_specs = (
        P("blk", "mer", "ply", None),
        P("blk", "mer", "ply", None),
        P("blk", "mer", "ply", None),
        P("blk", "mer", "ply", None),
        P("blk", "mer", "ply", None, None),
        P("blk", "mer", "ply", None),
        P(("blk", "mer", "ply"), None),
    )
    out_specs = (P("blk", "mer", "ply", None), P("blk", "mer", "ply", None))
    return jax.shard_map(
        functools.partial(local, sizes), mesh=mesh, in_specs=in_specs, out_specs=out_specs, check_vma=False
    )
```

```python
import functools

import jax
import jax.numpy as jnp
from jax import lax
from jax.experimental import pallas as pl
from jax.experimental.pallas import tpu as pltpu
from jax.sharding import PartitionSpec as P

ITERS = 4
EXCH = 2 * ITERS + 1
F32 = jnp.float32
BF16 = jnp.bfloat16
HIGH = lax.Precision.HIGHEST
MESH = pl.DeviceIdType.MESH
NT = (((1,), (1,)), ((), ()))


def halves(value):
    hi = value.astype(BF16)
    return hi, (value - hi.astype(F32)).astype(BF16)


def thirds(value):
    hi = value.astype(BF16)
    rest = value - hi.astype(F32)
    mid = rest.astype(BF16)
    return hi, mid, (rest - mid.astype(F32)).astype(BF16)


def dot(left, right):
    return jnp.dot(left, right, preferred_element_type=F32)


def remote(src, dst, send, recv, device):
    return pltpu.make_async_remote_copy(
        src_ref=src, dst_ref=dst, send_sem=send, recv_sem=recv, device_id=device, device_id_type=MESH
    )


def kernel(
    sizes,
    loads_ref, schur_ref, linv_ref, psi_ref, map_ref, list_ref, coarse_ref,
    x_ref, r_ref,
    lf, sf, lhi, llo, shi, slo,
    face_tx, face_rx, own, ply_rx,
    pdir, simg, mdir, upre, raw, acc, tb, perm, psc, pst,
    fwd_tx, far_tx, far_rx, pmap, nbr, dpad, wblk, chi, clo, lists, psn_tx, psn_rx, psn, tsm_tx, tsm_rx,
    sums, co1, ytx, co2, rz_ref, pap_ref,
    load_sem, face_ss, face_rs, ply_ss, ply_rs, fwd_ss, map_ss, map_rs,
    nbr_ss, nbr_rs, win_ss, win_rs, list_ss, list_rs,
    co1_ss, co1_rs, co2_ss, co2_rs, psn_ss, psn_rs, tsm_ss, tsm_rs, far_ss, far_rs,
):
    nb, nm, npl = sizes
    ng = nm * npl
    half, cases = loads_ref.shape
    face = half // 4
    owned = coarse_ref.shape[0]
    b = lax.axis_index("blk")
    m = lax.axis_index("mer")
    p = lax.axis_index("ply")
    q = 1 - p
    mp = m * npl + p
    b_prev = lax.rem(b + nb - 1, nb)
    b_next = lax.rem(b + 1, nb)
    has_lo = m > 0
    has_hi = m < nm - 1
    weight = [
        0.5,
        0.5,
        jnp.where(has_lo, 0.5, 1.0).astype(F32),
        jnp.where(has_hi, 0.5, 1.0).astype(F32),
    ]
    partner = (b, m, q)
    neighbour = [(b_prev, m, p), (b_next, m, p), (b, m - 1, p), (b, m + 1, p)]
    exists = [None, None, has_lo, has_hi]
    run = nb // 2
    place = lax.rem(b, run)
    first = jnp.where(place < run // 2, 0, 1)
    second = 1 - first
    at_end = jnp.logical_or(place == 0, place == run - 1)
    toward_end = (jnp.where(first == 0, b_prev, b_next), m, p)
    from_end = (jnp.where(first == 0, b_next, b_prev), m, p)
    across_end = (jnp.where(first == 0, b_prev, b_next), m, q)

    def device_at(f):
        if isinstance(f, int):
            return neighbour[f]
        return toward_end if f is first else from_end

    def opposite(f):
        return f ^ 1 if isinstance(f, int) else 1 - f

    def weight_of(f):
        return weight[f] if isinstance(f, int) else 0.5

    def guarded(f, fn):
        if not isinstance(f, int) or exists[f] is None:
            fn()
        else:
            pl.when(exists[f])(fn)

    mp_devices = [(b, i // npl, i % npl) for i in range(ng)]
    blk_devices = [(i, m, p) for i in range(nb)]

    def spread(me, devices, src_of, dst, send, recv):
        for i, device in enumerate(devices):
            pl.when(me != i)(lambda: remote(src_of(i), dst, send, recv, device).start())

    def fetch(index, source, side, target):
        column = pl.multiple_of(side * half, 128)
        return pltpu.make_async_copy(
            source.at[:, pl.ds(column, half)], target.at[index % 2], load_sem.at[index]
        )

    fetches = [
        fetch(0, linv_ref, p, lf),
        fetch(1, linv_ref, q, lf),
        fetch(2, schur_ref, p, sf),
        fetch(3, schur_ref, q, sf),
    ]
    for copy in fetches:
        copy.start()

    barrier = pltpu.get_barrier_semaphore()

    def greet(me, devices):
        for i, device in enumerate(devices):

            @pl.when(me != i)
            def _():
                pl.semaphore_signal(barrier, inc=1, device_id=device, device_id_type=MESH)

    greet(mp, mp_devices)
    greet(b, blk_devices)

    @pl.when(at_end)
    def _():
        pl.semaphore_signal(barrier, inc=1, device_id=across_end, device_id_type=MESH)

    rows = lax.broadcasted_iota(jnp.int32, (face, face), 0)
    for f in range(4):
        perm[f] = jnp.where(rows == map_ref[f : f + 1, :], 1.0, 0.0).astype(BF16)

    for f in (2, 3):

        @pl.when(jnp.logical_not(exists[f]))
        def _():
            def clear(e, carry):
                face_rx[e, f] = jnp.zeros((face, cases), F32)
                return carry

            lax.fori_loop(0, EXCH, clear, 0)
            nbr[1 + f] = jnp.zeros(nbr.shape[1:], F32)
            for it in range(ITERS):
                tsm_rx[it, f] = jnp.zeros((owned, cases), F32)

    map_copy = remote(map_ref, pmap, map_ss.at[0], map_rs.at[0], partner)

    lane = lax.broadcasted_iota(jnp.int32, (owned, lists.shape[2]), 1)
    sub = lax.broadcasted_iota(jnp.int32, (owned, lists.shape[2]), 0)
    mine = jnp.zeros_like(lane)
    for k in range(owned):
        mine = jnp.where(sub == k, list_ref[k], mine)
    lists[mp] = mine

    def permute(f, value):
        hi, mid, lo = thirds(value)
        out = dot(perm[f], jnp.concatenate([hi, mid, lo], axis=1))
        return (out[:, 2 * cases :] + out[:, cases : 2 * cases]) + out[:, :cases]

    def face_copy(e, f):
        there = opposite(f)
        return remote(
            face_tx.at[e, f], face_rx.at[e, there], face_ss.at[e, f], face_rs.at[e, there], device_at(f)
        )

    def face_send(e, f):
        def go():
            face_tx[e, f] = permute(f, raw[f])
            face_copy(e, f).start()

        guarded(f, go)

    def across_copy(e):
        return remote(face_tx.at[e, first], far_rx.at[e], far_ss.at[e], far_rs.at[e], across_end)

    def far_copy(e):
        return remote(far_tx.at[e], ply_rx.at[e, first], ply_ss.at[e, first], ply_rs.at[e, first], partner)

    def faces_send(e):
        @pl.when(at_end)
        def _():
            face_send(e, first)

            @pl.when(e < EXCH - 1)
            def _():
                across_copy(e).start()
                far_tx[e] = raw[first]
                far_copy(e).start()

        face_send(e, 2)
        face_send(e, 3)
        pl.when(jnp.logical_not(at_end))(lambda: face_send(e, first))
        face_send(e, second)

    def face_wait(e, f):
        guarded(
            f,
            lambda: remote(
                face_tx.at[e, f], face_rx.at[e, f], face_ss.at[e, f], face_rs.at[e, f], device_at(f)
            ).wait_recv(),
        )

    def faces_sent(e):
        for f in range(4):
            guarded(f, lambda f=f: face_copy(e, f).wait_send())

    def ply_copy(e, f):
        return remote(own.at[e, f], ply_rx.at[e, f], ply_ss.at[e, f], ply_rs.at[e, f], partner)

    def mer_forward(e):
        return remote(
            fwd_tx.at[e], ply_rx.at[e, 3], fwd_ss.at[e], ply_rs.at[e, 3], neighbour[2]
        )

    def when(condition, fn):
        pl.when(condition)(fn)

    def pass_mer(e):
        ply_copy(e, 2).wait_recv()

        @pl.when(has_lo)
        def _():
            fwd_tx[e] = permute(4, ply_rx[e, 2])
            mer_forward(e).start()

    def ply_sent(e):
        ply_copy(e, second).wait_send()
        ply_copy(e, 2).wait_send()
        when(jnp.logical_not(at_end), lambda: ply_copy(e, first).wait_send())

        @pl.when(at_end)
        def _():
            far_copy(e).wait_send()
            across_copy(e).wait_send()

        when(jnp.logical_not(has_hi), lambda: ply_copy(e, 3).wait_send())
        when(has_lo, lambda: mer_forward(e).wait_send())

    def batch(buffer, index, count, send, recv):
        block = buffer.at[index, pl.ds(0, count - 1)]
        return remote(block, block, send, recv, partner)

    def group_first(it, terms):
        co1[it, mp, pl.ds(0, owned)] = terms
        co1[it, mp, pl.ds(owned, 8)] = sums[...]
        spread(mp, mp_devices, lambda _: co1.at[it, mp], co1.at[it, mp], co1_ss.at[it], co1_rs.at[it])

    def group_second(it, coarse):
        batch(co1, it, ng, co1_ss.at[it], co1_rs.at[it]).wait_recv()
        if coarse:
            high, low = halves(co1[it, :, pl.ds(0, owned)].reshape(ng * owned, cases))
            both = dot(chi[...], jnp.concatenate([high, low], axis=1))
            y = (both[:, :cases] + both[:, cases:]) + dot(clo[...], high)
            ytx[it, :, pl.ds(0, owned)] = y.reshape(nb, owned, cases)
        else:
            ytx[it, :, pl.ds(0, owned)] = jnp.zeros((nb, owned, cases), F32)
        inner = jnp.sum(co1[it, :, pl.ds(owned, 8)], axis=0)
        ytx[it, :, pl.ds(owned, 8)] = jnp.broadcast_to(inner[None], (nb, 8, cases))
        spread(b, blk_devices, lambda i: ytx.at[it, i], co2.at[it, b], co2_ss.at[it], co2_rs.at[it])
        co2[it, b] = ytx[it, b]

    def group_end(it):
        batch(co2, it, nb, co2_ss.at[it], co2_rs.at[it]).wait_recv()
        total = jnp.sum(co2[it], axis=0)
        return total[:owned], total[owned : owned + 1], total[owned + 1 : owned + 2], total[owned + 2 : owned + 3]

    def group_sent(it):
        batch(co1, it, ng, co1_ss.at[it], co1_rs.at[it]).wait_send()
        batch(co2, it, nb, co2_ss.at[it], co2_rs.at[it]).wait_send()

    def rows_sum(value):
        return jnp.sum(value.reshape(face // 8, 8, cases), axis=0)

    def put_sums(parts):
        flat = [jnp.sum(part, axis=0, keepdims=True) for part in parts]
        index = lax.broadcasted_iota(jnp.int32, (8, cases), 0)
        out = jnp.zeros((8, cases), F32)
        for i, part in enumerate(flat):
            out = jnp.where(index == i, part, out)
        sums[...] = out

    def store_split(side, f, value):
        hi, lo = halves(value)
        tb[side, f, :, pl.ds(0, cases)] = hi
        tb[side, f, :, pl.ds(cases, cases)] = lo

    def product(hi, lo, side, pair):
        part = pl.ds(2 * pair * face, 2 * face)
        vector = tb[side, pl.ds(2 * pair, 2)].reshape(2 * face, 2 * cases)
        both = dot(hi[side, :, part], vector)
        small = dot(lo[side, :, part], vector[:, :cases])
        return ((both[:, :cases] + both[:, cases:]) + small).reshape(4, face, cases)

    def terms_copy(it, f):
        there = opposite(f)
        return remote(
            tsm_tx.at[it, f], tsm_rx.at[it, there], tsm_ss.at[it, f], tsm_rs.at[it, there], device_at(f)
        )

    def three_parts(value):
        return value[:owned, :cases] + value[:owned, cases:] + value[owned:, :cases]

    def terms_send(it):
        for f in range(4):
            store_split(1, f, weight[f] * raw[f])
        for f in (0, 1, 2, 3):

            def go():
                tsm_tx[it, f] = three_parts(dot(psn[f], tb[1, f]))
                terms_copy(it, f).start()

            guarded(f, go)
        co1[it, mp, pl.ds(0, owned)] = three_parts(dot(pst[...], tb[1].reshape(half, 2 * cases)))

    def terms_end(it):
        total = co1[it, mp, pl.ds(0, owned)]
        for f in (2, 3, 0, 1):
            guarded(
                f,
                lambda: remote(
                    tsm_tx.at[it, f], tsm_rx.at[it, f], tsm_ss.at[it, f], tsm_rs.at[it, f], device_at(f)
                ).wait_recv(),
            )
            total += tsm_rx[it, f]
        return total

    def terms_sent(it):
        for f in range(4):
            guarded(f, lambda f=f: terms_copy(it, f).wait_send())

    psi_hi, psi_lo = halves(psi_ref[...])
    psi_hi, psi_lo = psi_hi.astype(F32), psi_lo.astype(F32)
    pst[...] = jnp.concatenate([psi_hi, psi_lo], axis=0).astype(BF16)
    three = jnp.concatenate([psi_hi, psi_hi, psi_lo], axis=0).astype(BF16)
    eye_r = lax.broadcasted_iota(jnp.int32, (3 * owned, 3 * owned), 0)
    eye_c = lax.broadcasted_iota(jnp.int32, (3 * owned, 3 * owned), 1)
    eye = jnp.where(eye_r == eye_c, 1.0, 0.0).astype(BF16)
    psc[...] = lax.dot_general(
        three, eye, (((0,), (0,)), ((), ())), preferred_element_type=F32
    ).astype(BF16)

    def split_matrix(source, hi, lo):
        def step(i, carry):
            part = pl.ds(i * 64, 64)
            for side in range(2):
                a, c = halves(source[side, part, :])
                hi[side, part, :] = a
                lo[side, part, :] = c
            return carry

        lax.fori_loop(0, half // 64, step, 0)

    group = ng * owned
    this = (b * nm + m) * npl + p
    bases = [
        this * owned,
        ((b_prev * nm + m) * npl + p) * owned,
        ((b_next * nm + m) * npl + p) * owned,
        jnp.where(has_lo, (this - npl) * owned, -owned),
        jnp.where(has_hi, (this + npl) * owned, -owned),
    ]
    wide = lax.broadcasted_iota(jnp.int32, (owned, 5 * owned), 1)
    tall = lax.broadcasted_iota(jnp.int32, (owned, 5 * owned), 0)
    names = jnp.zeros_like(wide)
    for t in range(5):
        names = jnp.where(lax.div(wide, owned) == t, bases[t] + wide - t * owned, names)
    slots = jnp.zeros_like(wide)
    for k in range(owned):
        slots = jnp.where(tall == k, list_ref[k], slots)
    selector = jnp.where(slots == names, 1.0, 0.0).astype(F32)
    pl.semaphore_wait(barrier, ng - 1 + nb - 1 + jnp.where(at_end, 1, 0))

    slot_there = [2, 1, 4, 3]

    def nbr_copy(f):
        slot = slot_there[f]
        return remote(coarse_ref, nbr.at[slot], nbr_ss.at[f], nbr_rs.at[slot - 1], neighbour[f])

    for f in range(4):
        guarded(f, lambda f=f: nbr_copy(f).start())
    map_copy.start()
    nbr[0] = coarse_ref[...]
    spread(mp, mp_devices, lambda _: lists.at[mp], lists.at[mp], list_ss.at[0], list_rs.at[0])

    def psn_copy(f):
        there = opposite(f)
        return remote(psn_tx.at[f], psn_rx.at[there], psn_ss.at[f], psn_rs.at[there], device_at(f))

    for f in range(4):

        def go():
            hi, mid, lo = thirds(psi_ref[:, pl.ds(f * face, face)])
            stacked = jnp.concatenate(
                [hi.astype(F32), mid.astype(F32), lo.astype(F32)], axis=0
            ).astype(BF16)
            out = lax.dot_general(stacked, perm[f], NT, preferred_element_type=F32)
            psn_tx[f] = (out[2 * owned :] + out[owned : 2 * owned]) + out[:owned]
            psn_copy(f).start()

        guarded(f, go)

    for f in range(4):
        raw[f] = loads_ref[pl.ds(f * face, face), :]
    faces_send(0)

    for f in range(4):
        guarded(
            f,
            lambda f=f: remote(
                coarse_ref, nbr.at[1 + f], nbr_ss.at[f], nbr_rs.at[f], neighbour[f]
            ).wait_recv(),
        )
    hot = selector.astype(BF16)
    hi, mid, lo = thirds(nbr[...].reshape(5 * owned, nbr.shape[2]))
    named = (dot(hot, lo) + dot(hot, mid)) + dot(hot, hi)
    for j in range(nb + 2):
        block = (j - 1) % nb
        dpad[j] = named[:, block * group : (block + 1) * group]
    wblk[b] = dpad[pl.ds(b, 3)]
    spread(b, blk_devices, lambda peer: dpad.at[pl.ds(peer, 3)], wblk.at[b], win_ss.at[0], win_rs.at[0])

    for f in range(4):

        def go():
            remote(
                psn_tx.at[f], psn_rx.at[f], psn_ss.at[f], psn_rs.at[f], device_at(f)
            ).wait_recv()
            hi, lo = halves(psn_rx[f])
            psn[f] = jnp.concatenate([hi.astype(F32), lo.astype(F32)], axis=0).astype(BF16)

        guarded(f, go)
    terms_send(0)

    fetches[0].wait()
    fetches[1].wait()
    split_matrix(lf, lhi, llo)
    map_copy.wait_recv()
    perm[4] = jnp.where(rows == pmap[2:3, :], 1.0, 0.0).astype(BF16)
    for state in (x_ref, r_ref, pdir, simg, mdir, upre, pap_ref, sums):
        state[...] = jnp.zeros_like(state)
    rz_ref[...] = jnp.ones_like(rz_ref)

    def coarse_block():
        block = lists.at[pl.ds(0, ng - 1)]
        remote(block, block, list_ss.at[0], list_rs.at[0], partner).wait_recv()
        names = lists[:, :, pl.ds(0, group)].reshape(group, group)
        column = lax.broadcasted_iota(jnp.int32, (group, group), 1)
        block = wblk.at[pl.ds(0, nb - 1)]
        remote(block, block, win_ss.at[0], win_rs.at[0], partner).wait_recv()
        total = jnp.zeros((nb * owned, group), F32)
        for j, start in enumerate((b_prev, b, b_next)):
            hot = jnp.where(names == column + start * group, 1.0, 0.0).astype(BF16)
            window = wblk[:, j].reshape(nb * owned, group)
            hi, mid, lo = (
                lax.dot_general(piece, hot, NT, preferred_element_type=F32) for piece in thirds(window)
            )
            total += (lo + mid) + hi
        chi[...], clo[...] = halves(total)
        for f in range(4):
            guarded(f, lambda f=f: psn_copy(f).wait_send())
        for f in range(4):
            guarded(f, lambda f=f: nbr_copy(f).wait_send())
        block = lists.at[pl.ds(0, ng - 1)]
        remote(block, block, list_ss.at[0], list_rs.at[0], partner).wait_send()
        block = wblk.at[pl.ds(0, nb - 1)]
        remote(block, block, win_ss.at[0], win_rs.at[0], partner).wait_send()
        map_copy.wait_send()

    def assemble(e, f):
        face_wait(e, f)
        own[e, f] = raw[f] + face_rx[e, f]

    def exchange(e, hi, lo, weights, early, middle):
        def scaled(f, value):
            return value if weights is None else weight_of(f) * value

        def add(side, pair):
            acc[...] += product(hi, lo, side, pair)

        def pair_send(one, two):
            assemble(e, one)
            ply_copy(e, one).start()
            assemble(e, two)
            if isinstance(two, int):
                when(jnp.logical_not(has_hi), lambda: ply_copy(e, 3).start())
            else:
                ply_copy(e, two).start()

        def split(f):
            store_split(0, f, scaled(f, own[e, f]))

        early()
        pair_send(2, 3)
        split(2)
        split(3)
        acc[...] = product(hi, lo, 0, 1)

        @pl.when(jnp.logical_not(at_end))
        def _():
            pair_send(first, second)
            split(0)
            split(1)

        @pl.when(at_end)
        def _():
            assemble(e, second)
            ply_copy(e, second).start()
            split(second)

        middle()
        pass_mer(e)

        @pl.when(at_end)
        def _():
            assemble(e, first)
            split(first)

        add(0, 0)
        ply_copy(e, 3).wait_recv()
        for pair in (1, 0):
            if pair == 0:
                ply_copy(e, second).wait_recv()
                ply_copy(e, first).wait_recv()

                @pl.when(at_end)
                def _():
                    across_copy(e).wait_recv()
                    ply_rx[e, first] += far_rx[e]

            for f in (2 * pair, 2 * pair + 1):
                store_split(1, f, scaled(f, ply_rx[e, f]))
            add(1, pair)

    def steps(it, rz, energy, cross):
        beta = jnp.where(it <= 1, 0.0, rz / rz_ref[...])
        pap = (energy + 2.0 * beta * cross) + beta * beta * pap_ref[...]
        alpha = jnp.where(it == 0, -1.0, rz / pap)

        @pl.when(it > 0)
        def _():
            rz_ref[...] = rz
            pap_ref[...] = pap

        return alpha, beta

    def advance(e, alpha, beta):
        for f in range(4):
            part = pl.ds(f * face, face)
            value = own[e, f] + beta * simg[f]
            simg[f] = value
            r_ref[part, :] -= alpha * value

        @pl.when(e > 0)
        def _():
            for f in range(4):
                value = own[e - 1, f] + beta * pdir[f]
                pdir[f] = value
                x_ref[pl.ds(f * face, face), :] += alpha * value

    def iteration(it, carry):
        e1 = 2 * it
        e2 = e1 + 1

        def early():
            group_first(it, terms_end(it))

        def middle():
            @pl.when(it == 0)
            def _():
                coarse_block()

            group_second(it, True)

            @pl.when(it == 0)
            def _():
                fetches[2].wait()
                fetches[3].wait()
                split_matrix(sf, shi, slo)

        exchange(e1, lhi, llo, weight, early, middle)
        picked, rz, energy, cross = group_end(it)
        pick_hi = picked.astype(BF16).astype(F32)
        stack = jnp.concatenate([pick_hi, picked - pick_hi, pick_hi], axis=0).astype(BF16)
        correction = dot(psc[...], stack).reshape(4, face, cases)
        alpha, beta = steps(it, rz, energy, cross)
        for f in range(4):
            change = (acc[f] + correction[f]) + beta * mdir[f]
            mdir[f] = change
            value = upre[f] - alpha * change
            upre[f] = value
            raw[f] = weight[f] * value
        faces_send(e2)
        advance(e1, alpha, beta)
        partial = jnp.zeros((8, cases), F32)
        for f in range(4):
            partial += rows_sum(raw[f] * r_ref[pl.ds(f * face, face), :])
        faces_sent(e1)
        ply_sent(e1)
        group_sent(it)
        terms_sent(it)

        exchange(e2, shi, slo, None, lambda: None, lambda: None)
        raw[...] = acc[...]
        pl.when(it + 1 < ITERS)(lambda: terms_send(it + 1))
        faces_send(e2 + 1)
        energy = jnp.zeros((8, cases), F32)
        cross = jnp.zeros((8, cases), F32)
        for f in range(4):
            energy += rows_sum(raw[f] * own[e2, f])
            cross += rows_sum(raw[f] * pdir[f])
        put_sums((partial, energy, cross))
        faces_sent(e2)
        ply_sent(e2)
        return carry

    lax.fori_loop(0, ITERS, iteration, 0)

    last = EXCH - 1
    group_first(ITERS, jnp.zeros((owned, cases), F32))
    assemble(last, 2)
    assemble(last, 3)
    group_second(ITERS, False)
    assemble(last, 0)
    assemble(last, 1)
    _, rz, energy, cross = group_end(ITERS)
    alpha, beta = steps(ITERS, rz, energy, cross)
    advance(last, alpha, beta)
    faces_sent(last)
    group_sent(ITERS)


def deliver(x_ref, r_ref, x_out, r_out):
    x_out[...] = x_ref[...]
    r_out[...] = r_ref[...]


def local(sizes, loads, schur, local_inverse, psi, face_map, primal_list, coarse_inverse):
    nb, nm, npl = sizes
    ng = nm * npl
    half, cases = loads.shape[2:]
    face = half // 4
    owned, coarse = coarse_inverse.shape
    group = ng * owned
    shape = jax.ShapeDtypeStruct((half, cases), F32)
    vmem = pl.BlockSpec(memory_space=pltpu.VMEM)
    smem = pl.BlockSpec(memory_space=pltpu.SMEM)
    hbm = pl.BlockSpec(memory_space=pl.ANY)
    faces = (4, face, cases)
    dma = pltpu.SemaphoreType.DMA
    scratch = (
        [pltpu.VMEM((2, half, half), F32)] * 2
        + [pltpu.VMEM((2, half, half), BF16)] * 4
        + [pltpu.VMEM((EXCH,) + faces, F32)] * 4
        + [pltpu.VMEM(faces, F32)] * 5
        + [
            pltpu.VMEM(faces, F32),
            pltpu.VMEM((2, 4, face, 2 * cases), BF16),
            pltpu.VMEM((5, face, face), BF16),
            pltpu.VMEM((half, 3 * owned), BF16),
            pltpu.VMEM((2 * owned, half), BF16),
            pltpu.VMEM((EXCH, face, cases), F32),
            pltpu.VMEM((EXCH, face, cases), F32),
            pltpu.VMEM((EXCH, face, cases), F32),
            pltpu.VMEM((4, face), jnp.int32),
            pltpu.VMEM((5, owned, coarse), F32),
            pltpu.VMEM((nb + 2, owned, group), F32),
            pltpu.VMEM((nb, 3, owned, group), F32),
            pltpu.VMEM((nb * owned, group), BF16),
            pltpu.VMEM((nb * owned, group), BF16),
            pltpu.VMEM((ng, owned, 128), jnp.int32),
            pltpu.VMEM((4, owned, face), F32),
            pltpu.VMEM((4, owned, face), F32),
            pltpu.VMEM((4, 2 * owned, face), BF16),
            pltpu.VMEM((ITERS, 4, owned, cases), F32),
            pltpu.VMEM((ITERS, 4, owned, cases), F32),
            pltpu.VMEM((8, cases), F32),
            pltpu.VMEM((ITERS + 1, ng, owned + 8, cases), F32),
            pltpu.VMEM((ITERS + 1, nb, owned + 8, cases), F32),
            pltpu.VMEM((ITERS + 1, nb, owned + 8, cases), F32),
            pltpu.VMEM((1, cases), F32),
            pltpu.VMEM((1, cases), F32),
        ]
        + [dma((4,))]
        + [dma((EXCH, 4))] * 2
        + [dma((EXCH, 4))] * 2
        + [dma((EXCH,))]
        + [dma((1,))] * 2
        + [dma((4,))] * 2
        + [dma((1,))] * 4
        + [dma((ITERS + 1,))] * 4
        + [dma((4,))] * 2
        + [dma((ITERS, 4))] * 2
        + [dma((EXCH,))] * 2
    )
    x, r = pl.pallas_call(
        functools.partial(kernel, sizes),
        out_shape=(shape, shape),
        in_specs=[vmem, hbm, hbm, vmem, vmem, smem, vmem],
        out_specs=(vmem, vmem),
        scratch_shapes=scratch,
        compiler_params=pltpu.CompilerParams(
            collective_id=0, has_side_effects=True, vmem_limit_bytes=56 * 1024 * 1024
        ),
        name="bddc_cg",
    )(
        loads[0, 0],
        schur[0, 0],
        local_inverse[0, 0],
        psi[0, 0].T,
        face_map[0, 0, 0],
        primal_list[0, 0, 0],
        coarse_inverse,
    )
    x, r = pl.pallas_call(
        deliver,
        out_shape=(shape, shape),
        in_specs=[vmem, vmem],
        out_specs=(vmem, vmem),
        name="deliver",
    )(x, r)
    return x[None, None], r[None, None]


def solution(mesh):
    sizes = tuple(mesh.shape[axis] for axis in ("blk", "mer", "ply"))
    in_specs = (
        P("blk", "mer", "ply", None),
        P("blk", "mer", "ply", None),
        P("blk", "mer", "ply", None),
        P("blk", "mer", "ply", None),
        P("blk", "mer", "ply", None, None),
        P("blk", "mer", "ply", None),
        P(("blk", "mer", "ply"), None),
    )
    out_specs = (P("blk", "mer", "ply", None), P("blk", "mer", "ply", None))
    return jax.shard_map(
        functools.partial(local, sizes), mesh=mesh, in_specs=in_specs, out_specs=out_specs, check_vma=False
    )
```
